256 devices in a mesh: dom: 256 (over y, z, x, core).
Axes of the slice: x: 4, y: 4, z: 8, core: 2. Of those that a mesh axis runs over, the one named last changes fastest.
Arguments:
- right_side: float32 [16384, 32, 64], P('dom'), as said below
- a_blocks: float32 [16384, 7, 64, 64], P('dom'), as said below
- a_cols: int32 [16384, 6], P('dom'), may hold values from 0 to 95, as said below
- g_blocks: float32 [16384, 4, 64, 64], P('dom'), as said below
- g_cols: int32 [16384, 3], P('dom'), may hold values from 0 to 79, as said below
- send_up: int32 [256, 16], P('dom'), may hold values from 0 to 63, as said below
- send_down: int32 [256, 16], P('dom'), may hold values from 0 to 63, as said below
Outputs:
- solution: float32 [16384, 32, 64], P('dom')
- residual: float32 [16384, 32, 64], P('dom')
The draws below stay inside these ranges and needn't reach their ends.
Inputs may be any that keep to these rules, and one draw needn't show every extreme that they name: `a_cols`: neighbour columns of each block row in the order -x, +x, -y, +y, -z, +z of a periodic element grid: a value below 64 is an own block, 64 + h the h-th block from the device below, 80 + h the h-th block from the device above. `g_cols`: the -x, -y and -z columns of a_cols of the same row; a column is 64 or more exactly on the rows listed in send_down, and those rows' other columns are rows listed in send_down. `send_up`: for each device, 16 different local block indices. `send_down`: for each device, 16 different local block indices. `a_blocks`: the matrix is symmetric and positive definite: the couplings of two neighbouring rows are transposes of each other. `g_blocks`: the factor is nonsingular. `right_side`: Right-hand sides.
All inputs are finite; a program needn't handle non-finite values.
Results may differ from the reference program's by a relative error of at most 0.0005.
Values sent between devices are 32-bit elements; how exact they have to be, the bound alone decides.
A program may use at most 128 MiB of HBM per device.

```python
import jax
import jax.numpy as jnp
from jax import lax

DOFS = 64
RHS = 32
SX = 4
SY = 4
SZD = 4
ITERS = 3
FACE = 16
NB_DEV = 64
BLOCKS = 16384


def pick_rows_drawn(field, index):
    return field[index]


def shuffle_one(subkey):
    return jax.random.permutation(subkey, NB_DEV).astype(jnp.int32)


def local_order(key):
    devices = BLOCKS // NB_DEV
    keys = jax.random.split(key, devices)
    return jax.vmap(shuffle_one)(keys)


def neighbours(key):
    position = local_order(key)
    element = jnp.argsort(position, axis=1).astype(jnp.int32)
    coord_x = element % SX
    coord_y = element // SX % SY
    coord_z = element // FACE

    def local_of(ex, ey, ez):
        return jax.vmap(pick_rows_drawn)(position, ((ez * SY + ey) * SX + ex).astype(jnp.int32))
    left_x = local_of((coord_x - 1) % SX, coord_y, coord_z)
    right_x = local_of((coord_x + 1) % SX, coord_y, coord_z)
    left_y = local_of(coord_x, (coord_y - 1) % SY, coord_z)
    right_y = local_of(coord_x, (coord_y + 1) % SY, coord_z)
    face_index = coord_y * SX + coord_x
    below = jnp.where(coord_z > 0, local_of(coord_x, coord_y, jnp.maximum(coord_z - 1, 0)), NB_DEV + face_index)
    above = jnp.where(coord_z < SZD - 1, local_of(coord_x, coord_y, jnp.minimum(coord_z + 1, SZD - 1)), NB_DEV + FACE + face_index)
    return jnp.stack([left_x, right_x, left_y, right_y, below, above], axis=-1).astype(jnp.int32)


def draw_a_cols(key, part):
    return neighbours(key).reshape(BLOCKS, 6)


def draw_g_cols(key, part):
    return neighbours(key)[:, :, 0:5:2].reshape(BLOCKS, 3)


def draw_send_up(key, part):
    position = local_order(key)
    return position[:, (SZD - 1) * FACE:SZD * FACE]


def draw_send_down(key, part):
    position = local_order(key)
    return position[:, 0:FACE]


def draw_a_blocks(key, part):
    devices = BLOCKS // NB_DEV
    position = local_order(key)
    element = jnp.argsort(position, axis=1).astype(jnp.int32)
    key = jax.random.fold_in(key, 11)
    first, second, third = jax.random.split(key, 3)
    faces = jax.random.uniform(first, (devices, NB_DEV, 3, DOFS, DOFS), jnp.float32, -1.0, 0.2) / DOFS
    raw = jax.random.uniform(second, (devices, NB_DEV, DOFS, DOFS), jnp.float32, -1.0, 0.2) / DOFS
    symmetric = 0.5 * (raw + jnp.swapaxes(raw, -1, -2))
    diag_values = jax.random.uniform(third, (devices, NB_DEV, DOFS), jnp.float32, 7.5, 15.5)
    identity = jnp.eye(DOFS, dtype=jnp.float32)
    diag_block = symmetric * (1.0 - identity) + identity * diag_values[..., :, None]
    element_ids = jnp.arange(NB_DEV, dtype=jnp.int32)[None, :]
    device_ids = jnp.arange(devices, dtype=jnp.int32)[:, None]
    coord_x = element_ids % SX
    coord_y = element_ids // SX % SY
    coord_z = element_ids // FACE
    flat = faces.reshape(devices * NB_DEV, 3, DOFS, DOFS)
    left_x = device_ids * NB_DEV + (coord_z * SY + coord_y) * SX + (coord_x - 1) % SX
    left_y = device_ids * NB_DEV + (coord_z * SY + (coord_y - 1) % SY) * SX + coord_x
    left_z = jnp.where(coord_z > 0, device_ids * NB_DEV + element_ids - FACE, (device_ids - 1) % devices * NB_DEV + element_ids + (SZD - 1) * FACE)
    minus_x = jnp.swapaxes(flat[left_x, 0], -1, -2)
    minus_y = jnp.swapaxes(flat[left_y, 1], -1, -2)
    minus_z = jnp.swapaxes(flat[left_z, 2], -1, -2)
    ordered = jnp.stack([diag_block, minus_x, faces[:, :, 0], minus_y, faces[:, :, 1], minus_z, faces[:, :, 2]], axis=2)
    rows = jax.vmap(pick_rows_drawn)(ordered, element)
    return rows.reshape(BLOCKS, 7, DOFS, DOFS)


def draw_g_blocks(key, part):
    key = jax.random.fold_in(key, 12)
    first, second, third = jax.random.split(key, 3)
    raw = jax.random.uniform(first, (BLOCKS, 4, DOFS, DOFS), jnp.float32, -1.0, 1.0) * (0.2 / DOFS)
    diag_values = jax.random.uniform(second, (BLOCKS, DOFS), jnp.float32, 2.0, 4.0)
    coupling_diag = jax.random.uniform(third, (BLOCKS, 3, DOFS), jnp.float32, 0.15, 0.3)
    identity = jnp.eye(DOFS, dtype=jnp.float32)
    leading = raw[:, 0] * (1.0 - identity) + identity * diag_values[:, :, None]
    coupling = raw[:, 1:] + identity[None, None] * coupling_diag[:, :, :, None]
    return jnp.concatenate([leading[:, None], coupling], axis=1)


def draw_right_side(key, part):
    key = jax.random.fold_in(key, 13)
    first = jax.random.fold_in(key, 0)
    rising = 4.0 * jnp.power(3.0, jnp.arange(BLOCKS, dtype=jnp.float32) / BLOCKS)[:, None, None]
    owner = jnp.arange(BLOCKS, dtype=jnp.int32) // NB_DEV % 2
    alternate = (1.0 - 2.0 * owner.astype(jnp.float32))[:, None, None]
    values = jnp.clip(jax.random.normal(first, (BLOCKS, RHS, DOFS), jnp.float32), -6.0, 6.0) + alternate
    return values * rising


def setup_inputs(seed: int = 0) -> dict:
    splits = jax.random.split(jax.random.key(seed), 8)
    right_side = draw_right_side(jax.random.fold_in(splits[7], 71), 0)
    a_blocks = draw_a_blocks(jax.random.fold_in(splits[7], 71), 0)
    a_cols = draw_a_cols(jax.random.fold_in(splits[7], 71), 0)
    g_blocks = draw_g_blocks(jax.random.fold_in(splits[7], 71), 0)
    g_cols = draw_g_cols(jax.random.fold_in(splits[7], 71), 0)
    send_up = draw_send_up(jax.random.fold_in(splits[7], 71), 0)
    send_down = draw_send_down(jax.random.fold_in(splits[7], 71), 0)
    return {"right_side": right_side, "a_blocks": a_blocks, "a_cols": a_cols, "g_blocks": g_blocks, "g_cols": g_cols, "send_up": send_up, "send_down": send_down}


HIGH = lax.Precision.HIGHEST


def pick_rows(field, index):
    return field[index]


def add_rows(target, index, values):
    return target.at[index].add(values)


def block_product(diag_blocks, off_blocks, columns, extended, own_field):
    own_part = jnp.einsum('nab,nrb->nra', diag_blocks, own_field, precision=HIGH)
    nearby = extended[columns]
    return own_part + jnp.einsum('nkab,nkrb->nra', off_blocks, nearby, precision=HIGH)


def apply_matrix(field, a_blocks, a_cols, upper, lower):
    gathered = jax.vmap(pick_rows)
    extended = jnp.concatenate([field, jnp.roll(gathered(field, upper), 1, 0), jnp.roll(gathered(field, lower), -1, 0)], axis=1)

    def one_device(items):
        blocks, columns, wide, own_field = items
        return block_product(blocks[:, 0], blocks[:, 1:], columns, wide, own_field)

    return lax.map(one_device, (a_blocks, a_cols, extended, field))


def apply_precond(field, g_blocks, g_cols, upper):
    extended = jnp.concatenate([field, jnp.roll(jax.vmap(pick_rows)(field, upper), 1, 0)], axis=1)

    def forward_device(items):
        blocks, columns, wide, own_field = items
        return block_product(blocks[:, 0], blocks[:, 1:], columns, wide, own_field)

    values = lax.map(forward_device, (g_blocks, g_cols, extended, field))

    def transpose_device(items):
        blocks, columns, rows = items
        own_part = jnp.einsum('nab,nra->nrb', blocks[:, 0], rows, precision=HIGH)
        partial_terms = jnp.einsum('nkab,nra->nkrb', blocks[:, 1:], rows, precision=HIGH)
        buffer = jax.ops.segment_sum(partial_terms.reshape(-1, RHS, DOFS), columns.reshape(-1), num_segments=NB_DEV + FACE)
        return own_part + buffer[:NB_DEV], buffer[NB_DEV:]

    own_part, returned = lax.map(transpose_device, (g_blocks, g_cols, values))
    returned = jnp.roll(returned, -1, 0)
    return jax.vmap(add_rows)(own_part, upper, returned)


def inner_product(first, second):
    return jnp.sum(first * second, axis=(0, 1, 3))


def reference(right_side, a_blocks, a_cols, g_blocks, g_cols, send_up, send_down):
    devices = BLOCKS // NB_DEV
    field_shape = (devices, NB_DEV, RHS, DOFS)
    rhs_field = right_side.reshape(field_shape)
    a_split = a_blocks.reshape(devices, NB_DEV, 7, DOFS, DOFS)
    g_split = g_blocks.reshape(devices, NB_DEV, 4, DOFS, DOFS)
    a_lists = a_cols.reshape(devices, NB_DEV, 6)
    g_lists = g_cols.reshape(devices, NB_DEV, 3)
    solution = jnp.zeros(field_shape, jnp.float32)
    residual = rhs_field
    precond = apply_precond(residual, g_split, g_lists, send_up)
    rz_now = inner_product(residual, precond)
    direction = precond
    for iteration in range(ITERS):
        image = apply_matrix(direction, a_split, a_lists, send_up, send_down)
        alpha = rz_now / inner_product(direction, image)
        solution = solution + alpha[None, None, :, None] * direction
        residual = residual - alpha[None, None, :, None] * image
        if iteration + 1 < ITERS:
            precond = apply_precond(residual, g_split, g_lists, send_up)
            rz_next = inner_product(residual, precond)
            direction = precond + (rz_next / rz_now)[None, None, :, None] * direction
            rz_now = rz_next
    return solution.reshape(BLOCKS, RHS, DOFS), residual.reshape(BLOCKS, RHS, DOFS)
```

```python
import jax
import jax.numpy as jnp
from jax import lax
from jax.experimental import pallas as pl
from jax.experimental.pallas import tpu as pltpu
from jax.sharding import PartitionSpec as P

ROWS = 64
FACE = 16
LAYERS = 4
RHS = 32
DOFS = 64
MESH = pl.DeviceIdType.MESH
NT = (((1,), (1,)), ((), ()))
F32 = jnp.float32
BF16 = jnp.bfloat16
G_CHUNK = 16
A_CHUNK = 8
A_SLOTS = 4
GROUPS = ((1, 16), (16, 16))


def loop(lo, hi, fn, unroll=None):
    def step(i, carry):
        fn(i)
        return carry

    lax.fori_loop(lo, hi, step, 0, unroll=(hi - lo) if unroll is None else unroll)


def kernel(rhs_hbm, a_hbm, g_hbm, cols, send_up, send_down, x_hbm, r_hbm,
           rhs_in, a_in, g_in, a_w, g_w, gz_w, packed_w, packed_y, packed_m,
           low_w, high_y, low_m, high_m, y_loc, y_far,
           r0, u0, w0, m0, n0, u1, w1, m1, n1, x_out, r_out,
           gz_send, gz_recv, halo_send, halo_recv, dot_send, dot_recv,
           place, inverse, near, low_at, high_at, inverse_vec,
           in_sem, a_sem, out_sem, tab_sem, gz_ssem, gz_rsem, halo_ssem, halo_rsem, dot_ssem, dot_rsem):
    count = lax.axis_size("dom")
    me = lax.axis_index("dom")
    above = lax.rem(me + 1, count)
    below = lax.rem(me + count - 1, count)

    def partner(stride, size, step):
        mine = lax.rem(me // stride, size)
        return me + (lax.rem(mine + step, size) - mine) * stride

    def rhs_copy():
        return pltpu.make_async_copy(rhs_hbm, rhs_in, in_sem.at[0])

    def g_copy(c):
        part = pl.ds(c * G_CHUNK, G_CHUNK)
        return pltpu.make_async_copy(g_hbm.at[part], g_in.at[part], in_sem.at[1 + c])

    def a_copy(c):
        return pltpu.make_async_copy(a_hbm.at[pl.ds(c * A_CHUNK, A_CHUNK)], a_in.at[c % A_SLOTS], a_sem.at[c % A_SLOTS])

    rhs_copy().start()
    for c in range(ROWS // G_CHUNK):
        g_copy(c).start()
    for c in range(A_SLOTS):
        a_copy(c).start()

    barrier = pltpu.get_barrier_semaphore()
    greeted = 2
    for device in (above, below):
        pl.semaphore_signal(barrier, inc=1, device_id=(device,), device_id_type=MESH)
    for stride, size in GROUPS:
        for step in range(1, size):
            pl.semaphore_signal(barrier, inc=1, device_id=(partner(stride, size, step),), device_id_type=MESH)
            greeted += 1

    def first_layer(h):
        place[h] = send_down[0, h]

    loop(0, FACE, first_layer)

    def next_layer(e):
        place[e + FACE] = cols[5, place[e]]

    loop(0, ROWS - FACE, next_layer, 1)
    tab_lane = lax.broadcasted_iota(jnp.int32, (8, 128), 1)
    vec = lax.fori_loop(0, ROWS, lambda e, v: jnp.where(tab_lane == place[e], e, v),
                        jnp.zeros((8, 128), jnp.int32), unroll=8)
    inverse_vec[...] = vec
    tab = pltpu.make_async_copy(inverse_vec, inverse, tab_sem)
    tab.start()
    tab.wait()

    def neighbours(e):
        row = place[e]
        for k in range(4):
            near[e * 4 + k] = inverse[0, cols[k, row]]

    loop(0, ROWS, neighbours, 4)

    def crossings(h):
        low_at[h] = jnp.clip(cols[4, place[h]] - ROWS, 0, FACE - 1)
        high_at[h] = jnp.clip(cols[5, place[3 * FACE + h]] - (ROWS + FACE), 0, FACE - 1)

    loop(0, FACE, crossings, 4)

    left = lax.broadcasted_iota(jnp.int32, (RHS, 128), 1) < DOFS
    left2 = lax.broadcasted_iota(jnp.int32, (2 * RHS, 128), 1) < DOFS

    def twice(v):
        return jnp.concatenate([v, v], axis=1)

    def split(ref, e, v):
        hi = v.astype(BF16)
        ref[e, 0:RHS] = hi
        ref[e, RHS:2 * RHS] = (v - hi.astype(F32)).astype(BF16)

    def split_block(v):
        hi = v.astype(BF16)
        lo = (v - hi.astype(F32)).astype(BF16)
        return jnp.concatenate([hi, lo], axis=1)

    def times(fields, weights):
        out = lax.dot_general(jnp.concatenate(fields, axis=1), jnp.concatenate(weights, axis=1), NT,
                              preferred_element_type=F32)
        return out[:RHS] + out[RHS:]

    def times_transposed(fields, weights):
        pair = [jnp.where(left2, fields[0], fields[1]), jnp.where(left2, fields[2], fields[3])]
        out = jnp.dot(jnp.concatenate(pair, axis=1), jnp.concatenate(weights, axis=0), preferred_element_type=F32)
        out = out[:RHS] + out[RHS:]
        return out + pltpu.roll(out, DOFS, 1)

    def convert_g(c):
        g_copy(c).wait()

        def one(b):
            i = c * G_CHUNK + b // 4
            k = b % 4
            g_w[i * 4 + k] = split_block(g_in[i, k])

        loop(0, G_CHUNK * 4, one, 16)

    def convert_a(c):
        a_copy(c).wait()
        slot = c % A_SLOTS

        def one(i):
            for k in range(7):
                a_w[(c * A_CHUNK + i) * 7 + k] = split_block(a_in[slot, i, k])

        loop(0, A_CHUNK, one, 2)
        if c + A_SLOTS < ROWS // A_CHUNK:
            a_copy(c + A_SLOTS).start()

    def halo_copy(slot):
        return pltpu.make_async_remote_copy(
            src_ref=halo_send.at[slot], dst_ref=halo_recv.at[slot], send_sem=halo_ssem.at[slot],
            recv_sem=halo_rsem.at[slot], device_id=(above if slot % 2 == 0 else below,), device_id_type=MESH)

    def send_top(slot, field):
        def one(j):
            halo_send[slot, j] = jnp.where(left, field[inverse[0, send_up[0, 2 * j]]],
                                           field[inverse[0, send_up[0, 2 * j + 1]]])

        loop(0, FACE // 2, one)
        halo_copy(slot).start()

    def send_bottom(slot, field):
        def one(j):
            halo_send[slot, j] = jnp.where(left, field[2 * j], field[2 * j + 1])

        loop(0, FACE // 2, one)
        halo_copy(slot).start()

    def halves(v):
        turned = pltpu.roll(v, DOFS, 1)
        return jnp.where(left, v, turned), jnp.where(left, turned, v)

    def unpack_split(slot, ref):
        def one(j):
            first, second = halves(halo_recv[slot, j])
            split(ref, 2 * j, first)
            split(ref, 2 * j + 1, second)

        loop(0, FACE // 2, one)

    def row_y(e, below_block):
        row = place[e] * 4
        return times([packed_w[e], packed_w[near[e * 4]], packed_w[near[e * 4 + 2]], below_block],
                     [g_w[row], g_w[row + 1], g_w[row + 2], g_w[row + 3]])

    def row_u(e, above_block, above_weight):
        ex = near[e * 4 + 1]
        ey = near[e * 4 + 3]
        return times_transposed(
            [packed_y[e], packed_y[ex], packed_y[ey], above_block],
            [g_w[place[e] * 4], g_w[place[ex] * 4 + 1], g_w[place[ey] * 4 + 2], above_weight])

    def row_a(e, below_block, above_block):
        row = place[e] * 7
        return twice(times(
            [packed_m[e]] + [packed_m[near[e * 4 + k]] for k in range(4)] + [below_block, above_block],
            [a_w[row + k] for k in range(7)]))

    def product(number, field, out_m, out_n, beside_first, beside_second):
        base = number * 4
        send_top(base, field)

        def bottom(h):
            row = place[h] * 4
            v = times([packed_w[h], packed_w[near[h * 4]], packed_w[near[h * 4 + 2]]],
                      [g_w[row], g_w[row + 1], g_w[row + 2]])
            y_loc[h] = twice(v)

        loop(0, FACE, bottom)
        send_bottom(base + 1, y_loc)
        beside_first()

        def inner_y(e):
            split(packed_y, e, twice(row_y(e, packed_w[e - FACE])))

        loop(FACE, ROWS, inner_y)

        def put_u(e, v):
            out_m[e] = v
            split(packed_m, e, v)

        def inner_u(e):
            put_u(e, row_u(e, packed_y[e + FACE], g_w[place[e + FACE] * 4 + 3]))

        loop(FACE, 3 * FACE, inner_u)

        halo_copy(base).wait_recv()
        halo_copy(base + 1).wait_recv()
        unpack_split(base, low_w)

        def edge_y(j):
            pair = halves(halo_recv[base + 1, j])
            for s in range(2):
                y_far[2 * j + s] = pair[s]

        loop(0, FACE // 2, edge_y)

        def close_y(h):
            extra = times([low_w[low_at[h]]], [g_w[place[h] * 4 + 3]])
            split(packed_y, h, y_loc[h] + twice(extra))
            t = high_at[h]
            more = times([packed_w[3 * FACE + h]], [gz_w[t]])
            split(high_y, h, y_far[t] + twice(more))

        loop(0, FACE, close_y)

        def outer_u(h):
            put_u(h, row_u(h, packed_y[h + FACE], g_w[place[h + FACE] * 4 + 3]))
            e = 3 * FACE + h
            put_u(e, row_u(e, high_y[h], gz_w[high_at[h]]))

        loop(0, FACE, outer_u)
        send_bottom(base + 3, out_m)
        send_top(base + 2, out_m)
        beside_second()

        def inner_a(e):
            out_n[e] = row_a(e, packed_m[e - FACE], packed_m[e + FACE])

        loop(FACE, 3 * FACE, inner_a)
        halo_copy(base + 2).wait_recv()
        halo_copy(base + 3).wait_recv()
        unpack_split(base + 2, low_m)
        unpack_split(base + 3, high_m)

        def outer_a(h):
            out_n[h] = row_a(h, low_m[low_at[h]], packed_m[h + FACE])
            e = 3 * FACE + h
            out_n[e] = row_a(e, packed_m[e - FACE], high_m[high_at[h]])

        loop(0, FACE, outer_a)


    dot_lane = lax.broadcasted_iota(jnp.int32, (8, 128), 1)

    def dot_copies(number, stage):
        stride, size = GROUPS[stage]
        return [pltpu.make_async_remote_copy(
            src_ref=dot_send.at[number, stage], dst_ref=dot_recv.at[number, stage, step - 1],
            send_sem=dot_ssem.at[number, stage], recv_sem=dot_rsem.at[number, stage],
            device_id=(partner(stride, size, step),), device_id_type=MESH) for step in range(1, size)]

    def dot_start(number, stage, value):
        dot_send[number, stage] = value
        for c in dot_copies(number, stage):
            c.start()

    def dot_finish(number, stage):
        slots = dot_recv.at[number, stage]
        pltpu.make_async_copy(slots, slots, dot_rsem.at[number, stage]).wait()
        return dot_send[number, stage] + jnp.sum(dot_recv[number, stage], axis=0)

    def dot_pack(first, second):
        first = jnp.sum(first, axis=1, keepdims=True)
        second = jnp.sum(second, axis=1, keepdims=True)
        out = jnp.zeros((8, 128), F32)
        for g in range(4):
            out = jnp.where(dot_lane == 2 * g, first[8 * g:8 * g + 8], out)
            out = jnp.where(dot_lane == 2 * g + 1, second[8 * g:8 * g + 8], out)
        return out

    def dot_unpack(v):
        first = jnp.concatenate([v[:, 2 * g:2 * g + 1] for g in range(4)], axis=0)
        second = jnp.concatenate([v[:, 2 * g + 1:2 * g + 2] for g in range(4)], axis=0)
        return first, second

    zero = jnp.zeros((RHS, 128), F32)

    rhs_copy().wait()

    def load_rhs(e):
        v = twice(rhs_in[place[e]])
        r0[e] = v
        split(packed_w, e, v)

    loop(0, ROWS, load_rhs, 16)
    for c in range(ROWS // G_CHUNK):
        convert_g(c)
    pl.semaphore_wait(barrier, greeted)

    def gz_copy():
        return pltpu.make_async_remote_copy(src_ref=gz_send, dst_ref=gz_recv, send_sem=gz_ssem, recv_sem=gz_rsem,
                                            device_id=(below,), device_id_type=MESH)

    def fill_gz(j):
        gz_send[j] = jnp.concatenate([g_in[place[2 * j], 3], g_in[place[2 * j + 1], 3]], axis=1)

    def first_side():
        loop(0, FACE // 2, fill_gz)
        gz_copy().start()
        for c in range(ROWS // A_CHUNK - 2):
            convert_a(c)
        gz_copy().wait_recv()

        def one(j):
            v = gz_recv[j]
            gz_w[2 * j] = split_block(v[:, :DOFS])
            gz_w[2 * j + 1] = split_block(v[:, DOFS:])

        loop(0, FACE // 2, one)

    def second_side():
        for c in range(ROWS // A_CHUNK - 2, ROWS // A_CHUNK):
            convert_a(c)

    product(0, r0, u0, w0, first_side, second_side)

    def dots0(e, carry):
        split(packed_w, e, w0[e])
        return carry[0] + r0[e] * u0[e], carry[1] + w0[e] * u0[e]

    value = dot_pack(*lax.fori_loop(0, ROWS, dots0, (zero, zero), unroll=16))
    dot_start(0, 0, value)

    def middle(number):
        def run():
            dot_start(number, 1, dot_finish(number, 0))
        return run

    def nothing():
        pass

    product(1, w0, m0, n0, nothing, middle(0))
    gam0, del0 = dot_unpack(dot_finish(0, 1))
    alpha0 = gam0 / del0
    al0 = jnp.broadcast_to(alpha0, (RHS, 128))

    def update0(e, carry):
        u = u0[e] - al0 * m0[e]
        w = w0[e] - al0 * n0[e]
        r = r0[e] - al0 * w0[e]
        u1[e] = u
        w1[e] = w
        split(packed_w, e, w)
        return carry[0] + r * u, carry[1] + w * u

    value = dot_pack(*lax.fori_loop(0, ROWS, update0, (zero, zero), unroll=16))
    dot_start(1, 0, value)

    product(2, w1, m1, n1, nothing, middle(1))
    gam1, del1 = dot_unpack(dot_finish(1, 1))
    beta1 = gam1 / gam0
    alpha1 = gam1 / (del1 - beta1 * gam1 / alpha0)
    al1 = jnp.broadcast_to(alpha1, (RHS, 128))
    ab1 = jnp.broadcast_to(alpha1 * beta1, (RHS, 128))
    be1 = jnp.broadcast_to(beta1, (RHS, 128))
    k0 = jnp.broadcast_to(alpha0 + alpha1 * beta1, (RHS, 128))

    def update1(e, carry):
        u = u1[e] - (al1 * m1[e] + ab1 * m0[e])
        w = w1[e] - (al1 * n1[e] + ab1 * n0[e])
        r = r0[e] - (k0 * w0[e] + al1 * w1[e])
        m1[e] = u
        n1[e] = w
        return carry[0] + r * u, carry[1] + w * u

    value = dot_pack(*lax.fori_loop(0, ROWS, update1, (zero, zero), unroll=16))
    dot_start(2, 0, value)

    def prepare(e):
        u, w = u0[e], w0[e]
        v, q = u1[e], w1[e]
        m0[e] = k0 * u + al1 * v
        u0[e] = v + be1 * u
        n0[e] = r0[e] - (k0 * w + al1 * q)
        w0[e] = q + be1 * w

    loop(0, ROWS, prepare, 16)
    dot_start(2, 1, dot_finish(2, 0))
    gam2, del2 = dot_unpack(dot_finish(2, 1))
    beta2 = gam2 / gam1
    alpha2 = gam2 / (del2 - beta2 * gam2 / alpha1)
    al2 = jnp.broadcast_to(alpha2, (RHS, 128))
    ab2 = jnp.broadcast_to(alpha2 * beta2, (RHS, 128))

    def finish_x(i):
        e = inverse[0, i]
        x_out[i] = (m0[e] + (al2 * m1[e] + ab2 * u0[e]))[:, :DOFS]

    def finish_r(i):
        e = inverse[0, i]
        r_out[i] = (n0[e] - (al2 * n1[e] + ab2 * w0[e]))[:, :DOFS]

    loop(0, ROWS, finish_x, 16)
    x_copy = pltpu.make_async_copy(x_out, x_hbm, out_sem.at[0])
    x_copy.start()
    loop(0, ROWS, finish_r, 16)
    r_copy = pltpu.make_async_copy(r_out, r_hbm, out_sem.at[1])
    r_copy.start()
    x_copy.wait()
    r_copy.wait()

    gz_copy().wait_send()
    for slot in range(12):
        halo_copy(slot).wait_send()
    for number in range(3):
        for stage in range(2):
            slots = dot_recv.at[number, stage]
            pltpu.make_async_copy(slots, slots, dot_ssem.at[number, stage]).wait()


def body(right_side, a_blocks, a_cols, g_blocks, g_cols, send_up, send_down):
    field = pltpu.VMEM((ROWS, RHS, 128), F32)
    packed = pltpu.VMEM((ROWS, 2 * RHS, 128), BF16)
    face = pltpu.VMEM((FACE, 2 * RHS, 128), BF16)
    hbm = pl.BlockSpec(memory_space=pl.ANY)
    smem = pl.BlockSpec(memory_space=pltpu.SMEM)
    dma = pltpu.SemaphoreType.DMA
    out = jax.ShapeDtypeStruct((ROWS, RHS, DOFS), F32)
    return pl.pallas_call(
        kernel,
        out_shape=(out, out),
        in_specs=[hbm, hbm, hbm, smem, smem, smem],
        out_specs=(hbm, hbm),
        scratch_shapes=[
            pltpu.VMEM((ROWS, RHS, DOFS), F32),
            pltpu.VMEM((A_SLOTS, A_CHUNK, 7, DOFS, DOFS), F32),
            pltpu.VMEM((ROWS, 4, DOFS, DOFS), F32),
            pltpu.VMEM((ROWS * 7, DOFS, 128), BF16),
            pltpu.VMEM((ROWS * 4, DOFS, 128), BF16),
            pltpu.VMEM((FACE, DOFS, 128), BF16),
            packed, packed, packed,
            face, face, face, face,
            pltpu.VMEM((FACE, RHS, 128), F32),
            pltpu.VMEM((FACE, RHS, 128), F32),
            field, field, field, field, field, field, field, field, field,
            pltpu.VMEM((ROWS, RHS, DOFS), F32),
            pltpu.VMEM((ROWS, RHS, DOFS), F32),
            pltpu.VMEM((FACE // 2, DOFS, 128), F32),
            pltpu.VMEM((FACE // 2, DOFS, 128), F32),
            pltpu.VMEM((12, FACE // 2, RHS, 128), F32),
            pltpu.VMEM((12, FACE // 2, RHS, 128), F32),
            pltpu.VMEM((3, 2, 8, 128), F32),
            pltpu.VMEM((3, 2, 15, 8, 128), F32),
            pltpu.SMEM((ROWS,), jnp.int32),
            pltpu.SMEM((8, 128), jnp.int32),
            pltpu.SMEM((ROWS * 4,), jnp.int32),
            pltpu.SMEM((FACE,), jnp.int32),
            pltpu.SMEM((FACE,), jnp.int32),
            pltpu.VMEM((8, 128), jnp.int32),
            dma((5,)), dma((A_SLOTS,)), dma((2,)), dma, dma, dma,
            dma((12,)), dma((12,)), dma((3, 2)), dma((3, 2)),
        ],
        compiler_params=pltpu.CompilerParams(
            collective_id=0, has_side_effects=True, vmem_limit_bytes=60 * 2 ** 20),
    )(right_side, a_blocks, g_blocks, a_cols.T, send_up, send_down)


def solution(mesh):
    in_specs = (
        P("dom", None, None),
        P("dom", None, None, None),
        P("dom", None),
        P("dom", None, None, None),
        P("dom", None),
        P("dom", None),
        P("dom", None),
    )
    out_specs = (P("dom", None, None), P("dom", None, None))
    return jax.shard_map(body, mesh=mesh, in_specs=in_specs, out_specs=out_specs, check_vma=False)
```

```python
import itertools

import jax
import jax.numpy as jnp
from jax import lax
from jax.experimental import pallas as pl
from jax.experimental.pallas import tpu as pltpu
from jax.sharding import PartitionSpec as P

ROWS = 64
FACE = 16
LAYERS = 4
RHS = 32
DOFS = 64
MESH = pl.DeviceIdType.MESH
NT = (((1,), (1,)), ((), ()))
F32 = jnp.float32
BF16 = jnp.bfloat16
G_CHUNK = 16
A_CHUNK = 8
A_SLOTS = 4
GROUPS = (((1, 2), (2, 4), (64, 4)), ((8, 8),))
FIRST_SLOT = (0, 31, 38)


def loop(lo, hi, fn, unroll=None):
    def step(i, carry):
        fn(i)
        return carry

    lax.fori_loop(lo, hi, step, 0, unroll=(hi - lo) if unroll is None else unroll)


def kernel(rhs_hbm, a_hbm, g_hbm, cols, send_up, send_down, parts_hbm, alpha_hbm, alpha_beta_hbm,
           rhs_in, a_in, g_in, a_w, g_w, gz_w, g0_w, packed_w, packed_y, packed_m,
           low_w, high_y, low_m, high_m, low_t, high_t, y_loc, y_far, u_low, u_high,
           r0, u0, w0, m0, n0, u1, w1, m1, n1, parts, coef,
           gz_send, gz_recv, g0_send, g0_recv, halo_send, halo_recv, dot_send, dot_recv,
           place, inverse, near, low_at, high_at, low_side, high_side, inverse_vec,
           in_sem, a_sem, out_sem, tab_sem, gz_ssem, gz_rsem, g0_ssem, g0_rsem, halo_ssem, halo_rsem, dot_ssem, dot_rsem):
    count = lax.axis_size("dom")
    me = lax.axis_index("dom")
    above = lax.rem(me + 1, count)
    below = lax.rem(me + count - 1, count)

    def partners(stage):
        out = []
        for steps in itertools.product(*[range(size) for _, size in GROUPS[stage]]):
            device = me
            for (stride, size), step in zip(GROUPS[stage], steps):
                if step:
                    mine = lax.rem(me // stride, size)
                    device = device + (lax.rem(mine + step, size) - mine) * stride
            if any(steps):
                out.append(device)
        return out

    def rhs_copy():
        return pltpu.make_async_copy(rhs_hbm, rhs_in, in_sem.at[0])

    def g_copy(c):
        part = pl.ds(c * G_CHUNK, G_CHUNK)
        return pltpu.make_async_copy(g_hbm.at[part], g_in.at[part], in_sem.at[1 + c])

    def a_copy(c):
        return pltpu.make_async_copy(a_hbm.at[pl.ds(c * A_CHUNK, A_CHUNK)], a_in.at[c % A_SLOTS], a_sem.at[c % A_SLOTS])

    rhs_copy().start()
    for c in range(ROWS // G_CHUNK):
        g_copy(c).start()
    for c in range(A_SLOTS):
        a_copy(c).start()

    barrier = pltpu.get_barrier_semaphore()
    greeted = 2
    for device in (above, below):
        pl.semaphore_signal(barrier, inc=1, device_id=(device,), device_id_type=MESH)
    for stage in range(2):
        for device in partners(stage):
            pl.semaphore_signal(barrier, inc=1, device_id=(device,), device_id_type=MESH)
            greeted += 1

    def first_layer(h):
        place[h] = send_down[0, h]

    loop(0, FACE, first_layer)

    def next_layer(e):
        place[e + FACE] = cols[5, place[e]]

    loop(0, ROWS - FACE, next_layer, 1)
    tab_lane = lax.broadcasted_iota(jnp.int32, (8, 128), 1)
    vec = lax.fori_loop(0, ROWS, lambda e, v: jnp.where(tab_lane == place[e], e, v),
                        jnp.zeros((8, 128), jnp.int32), unroll=8)
    inverse_vec[...] = vec
    tab = pltpu.make_async_copy(inverse_vec, inverse, tab_sem)
    tab.start()
    tab.wait()

    def neighbours(e):
        row = place[e]
        for k in range(4):
            near[e * 4 + k] = inverse[0, cols[k, row]]

    loop(0, ROWS, neighbours, 4)

    def crossings(h):
        low_at[h] = jnp.clip(cols[4, place[h]] - ROWS, 0, FACE - 1)
        high_at[h] = jnp.clip(cols[5, place[3 * FACE + h]] - (ROWS + FACE), 0, FACE - 1)

        for s in range(2):
            low_side[h * 2 + s] = jnp.clip(near[h * 4 + 1 + 2 * s], 0, FACE - 1)
            high_side[h * 2 + s] = jnp.clip(near[(3 * FACE + h) * 4 + 1 + 2 * s] - 3 * FACE, 0, FACE - 1)

    loop(0, FACE, crossings, 4)

    left = lax.broadcasted_iota(jnp.int32, (RHS, 128), 1) < DOFS
    left2 = lax.broadcasted_iota(jnp.int32, (2 * RHS, 128), 1) < DOFS

    def twice(v):
        return jnp.concatenate([v, v], axis=1)

    def split(ref, e, v):
        hi = v.astype(BF16)
        ref[e, 0:RHS] = hi
        ref[e, RHS:2 * RHS] = (v - hi.astype(F32)).astype(BF16)

    def split_block(v):
        hi = v.astype(BF16)
        lo = (v - hi.astype(F32)).astype(BF16)
        return jnp.concatenate([hi, lo], axis=1)

    def times(fields, weights):
        out = lax.dot_general(jnp.concatenate(fields, axis=1), jnp.concatenate(weights, axis=1), NT,
                              preferred_element_type=F32)
        return out[:RHS] + out[RHS:]

    def times_transposed(fields, weights):
        pair = [jnp.where(left2, fields[i], fields[i + 1]) for i in range(0, len(fields) - 1, 2)]
        if len(fields) % 2:
            pair.append(fields[-1][:, :DOFS])
        out = jnp.dot(jnp.concatenate(pair, axis=1), jnp.concatenate(weights, axis=0), preferred_element_type=F32)
        out = out[:RHS] + out[RHS:]
        return out + pltpu.roll(out, DOFS, 1)

    def convert_g(c):
        def one(b):
            i = c * G_CHUNK + b // 4
            k = b % 4
            g_w[i * 4 + k] = split_block(g_in[i, k])

        loop(0, G_CHUNK * 4, one)

    def convert_a(c):
        a_copy(c).wait()
        slot = c % A_SLOTS

        def one(i):
            for k in range(7):
                a_w[(c * A_CHUNK + i) * 7 + k] = split_block(a_in[slot, i, k])

        loop(0, A_CHUNK, one)
        if c + A_SLOTS < ROWS // A_CHUNK:
            a_copy(c + A_SLOTS).start()

    def halo_copy(slot):
        return pltpu.make_async_remote_copy(
            src_ref=halo_send.at[slot], dst_ref=halo_recv.at[slot], send_sem=halo_ssem.at[slot],
            recv_sem=halo_rsem.at[slot], device_id=(above if slot % 2 == 0 else below,), device_id_type=MESH)

    def send_top(slot, field):
        def one(j):
            halo_send[slot, j] = jnp.where(left, field[inverse[0, send_up[0, 2 * j]]],
                                           field[inverse[0, send_up[0, 2 * j + 1]]])

        loop(0, FACE // 2, one)
        halo_copy(slot).start()

    def send_bottom(slot, field):
        def one(j):
            halo_send[slot, j] = jnp.where(left, field[2 * j], field[2 * j + 1])

        loop(0, FACE // 2, one)
        halo_copy(slot).start()

    def halves(v):
        turned = pltpu.roll(v, DOFS, 1)
        return jnp.where(left, v, turned), jnp.where(left, turned, v)

    def unpack(slot, ref):
        def one(j):
            ref[2 * j], ref[2 * j + 1] = halves(halo_recv[slot, j])

        loop(0, FACE // 2, one)

    def unpack_split(slot, ref):
        def one(j):
            first, second = halves(halo_recv[slot, j])
            split(ref, 2 * j, first)
            split(ref, 2 * j + 1, second)

        loop(0, FACE // 2, one)

    def row_y(e, below_block):
        row = place[e] * 4
        return times([packed_w[e], packed_w[near[e * 4]], packed_w[near[e * 4 + 2]], below_block],
                     [g_w[row], g_w[row + 1], g_w[row + 2], g_w[row + 3]])

    def row_u(e, above_block, above_weight):
        ex = near[e * 4 + 1]
        ey = near[e * 4 + 3]
        return times_transposed(
            [packed_y[e], packed_y[ex], packed_y[ey], above_block],
            [g_w[place[e] * 4], g_w[place[ex] * 4 + 1], g_w[place[ey] * 4 + 2], above_weight])

    def row_a(e, below_block, above_block):
        row = place[e] * 7
        return twice(times(
            [packed_m[e]] + [packed_m[near[e * 4 + k]] for k in range(4)] + [below_block, above_block],
            [a_w[row + k] for k in range(7)]))

    def bottom(h):
        row = place[h] * 4
        v = twice(times([packed_w[h], packed_w[near[h * 4]], packed_w[near[h * 4 + 2]]],
                        [g_w[row], g_w[row + 1], g_w[row + 2]]))
        y_loc[h] = v
        split(packed_y, h, v)

    def inner_y(e):
        split(packed_y, e, twice(row_y(e, packed_w[e - FACE])))

    def first_product(field, out_m, out_n, beside_first, beside_second):
        loop(0, FACE, bottom)
        send_bottom(1, y_loc)
        beside_first()
        loop(FACE, ROWS, inner_y)

        def put_u(e, v):
            out_m[e] = v
            split(packed_m, e, v)

        def inner_u(e):
            put_u(e, row_u(e, packed_y[e + FACE], g_w[place[e + FACE] * 4 + 3]))

        loop(FACE, 3 * FACE, inner_u)
        halo_copy(0).wait_recv()
        halo_copy(1).wait_recv()
        unpack_split(0, low_w)
        unpack(1, y_far)

        def close_y(h):
            extra = times([low_w[low_at[h]]], [g_w[place[h] * 4 + 3]])
            split(packed_y, h, y_loc[h] + twice(extra))
            t = high_at[h]
            more = times([packed_w[3 * FACE + h]], [gz_w[t]])
            split(high_y, h, y_far[t] + twice(more))

        loop(0, FACE, close_y)

        def outer_u(h):
            put_u(h, row_u(h, packed_y[h + FACE], g_w[place[h + FACE] * 4 + 3]))
            e = 3 * FACE + h
            put_u(e, row_u(e, high_y[h], gz_w[high_at[h]]))

        loop(0, FACE, outer_u)
        send_bottom(3, out_m)
        send_top(2, out_m)
        beside_second()

        def inner_a(e):
            out_n[e] = row_a(e, packed_m[e - FACE], packed_m[e + FACE])

        loop(FACE, 3 * FACE, inner_a)
        halo_copy(2).wait_recv()
        halo_copy(3).wait_recv()
        unpack_split(2, low_m)
        unpack_split(3, high_m)

        def outer_a(h):
            out_n[h] = row_a(h, low_m[low_at[h]], packed_m[h + FACE])
            e = 3 * FACE + h
            out_n[e] = row_a(e, packed_m[e - FACE], high_m[high_at[h]])

        loop(0, FACE, outer_a)

    def later_product(number, field, out_m, out_n, beside):
        base = number * 4
        send_top(base, field)
        loop(0, FACE, bottom)
        send_bottom(base + 1, y_loc)
        loop(FACE, 2 * FACE, inner_y)
        loop(3 * FACE, ROWS, inner_y)

        def part_u(h):
            out_m[h] = row_u(h, packed_y[h + FACE], g_w[place[h + FACE] * 4 + 3])
            e = 3 * FACE + h
            ex = near[e * 4 + 1]
            ey = near[e * 4 + 3]
            out_m[e] = times_transposed([packed_y[e], packed_y[ex], packed_y[ey]],
                                        [g_w[place[e] * 4], g_w[place[ex] * 4 + 1], g_w[place[ey] * 4 + 2]])

        loop(0, FACE, part_u)
        send_bottom(base + 3, out_m)
        send_top(base + 2, out_m)
        loop(2 * FACE, 3 * FACE, inner_y)

        def put_u(e, v):
            out_m[e] = v
            split(packed_m, e, v)

        def inner_u(e):
            put_u(e, row_u(e, packed_y[e + FACE], g_w[place[e + FACE] * 4 + 3]))

        loop(FACE, 3 * FACE, inner_u)

        def part_a(h):
            for layer, k, other in ((1, 6, 2), (2, 5, 1)):
                e = layer * FACE + h
                row = place[e] * 7
                out_n[e] = twice(times(
                    [packed_m[e]] + [packed_m[near[e * 4 + i]] for i in range(4)] + [packed_m[other * FACE + h]],
                    [a_w[row + i] for i in range(5)] + [a_w[row + k]]))

        loop(0, FACE, part_a)
        beside()
        halo_copy(base).wait_recv()
        halo_copy(base + 1).wait_recv()
        unpack_split(base, low_w)
        unpack(base + 1, y_far)

        def close_y(h):
            extra = twice(times([low_w[low_at[h]]], [g_w[place[h] * 4 + 3]]))
            split(low_t, h, extra)
            split(packed_y, h, y_loc[h] + extra)
            t = high_at[h]
            more = twice(times([packed_w[3 * FACE + h]], [gz_w[t]]))
            split(high_t, h, more)
            split(high_y, h, y_far[t] + more)

        loop(0, FACE, close_y)
        halo_copy(base + 2).wait_recv()
        halo_copy(base + 3).wait_recv()
        unpack(base + 2, u_low)
        unpack(base + 3, u_high)

        def close_u(h):
            ex, ey = low_side[2 * h], low_side[2 * h + 1]
            put_u(h, out_m[h] + times_transposed(
                [low_t[h], low_t[ex], low_t[ey]],
                [g_w[place[h] * 4], g_w[place[ex] * 4 + 1], g_w[place[ey] * 4 + 2]]))
            e = 3 * FACE + h
            put_u(e, out_m[e] + times_transposed([high_y[h]], [gz_w[high_at[h]]]))
            split(low_m, h, u_low[low_at[h]] + times_transposed([packed_y[h]], [g_w[place[h] * 4 + 3]]))
            hx, hy = high_side[2 * h], high_side[2 * h + 1]
            split(high_m, h, u_high[high_at[h]] + times_transposed(
                [high_t[h], high_t[hx], high_t[hy]],
                [g0_w[high_at[h] * 3], g0_w[high_at[hx] * 3 + 1], g0_w[high_at[hy] * 3 + 2]]))

        loop(0, FACE, close_u)

        def close_a(h):
            out_n[h] = row_a(h, low_m[h], packed_m[h + FACE])
            e = 3 * FACE + h
            out_n[e] = row_a(e, packed_m[e - FACE], high_m[h])
            for layer, k, other in ((1, 5, 0), (2, 6, 3)):
                e = layer * FACE + h
                out_n[e] = out_n[e] + twice(times([packed_m[other * FACE + h]], [a_w[place[e] * 7 + k]]))

        loop(0, FACE, close_a)

    dot_lane = lax.broadcasted_iota(jnp.int32, (8, 128), 1)

    def dot_slots(number, stage):
        return dot_recv.at[number, pl.ds(FIRST_SLOT[stage], FIRST_SLOT[stage + 1] - FIRST_SLOT[stage])]

    def dot_start(number, stage, value):
        dot_send[number, stage] = value
        for i, device in enumerate(partners(stage)):
            pltpu.make_async_remote_copy(
                src_ref=dot_send.at[number, stage], dst_ref=dot_recv.at[number, FIRST_SLOT[stage] + i],
                send_sem=dot_ssem.at[number, stage], recv_sem=dot_rsem.at[number, stage],
                device_id=(device,), device_id_type=MESH).start()

    def dot_finish(number, stage):
        slots = dot_slots(number, stage)
        pltpu.make_async_copy(slots, slots, dot_rsem.at[number, stage]).wait()
        got = dot_recv[number, FIRST_SLOT[stage]:FIRST_SLOT[stage + 1]]
        return dot_send[number, stage] + jnp.sum(got, axis=0)

    def dot_pack(first, second):
        first = jnp.sum(first, axis=1, keepdims=True)
        second = jnp.sum(second, axis=1, keepdims=True)
        out = jnp.zeros((8, 128), F32)
        for g in range(4):
            out = jnp.where(dot_lane == 2 * g, first[8 * g:8 * g + 8], out)
            out = jnp.where(dot_lane == 2 * g + 1, second[8 * g:8 * g + 8], out)
        return out

    def dot_unpack(v):
        first = jnp.concatenate([v[:, 2 * g:2 * g + 1] for g in range(4)], axis=0)
        second = jnp.concatenate([v[:, 2 * g + 1:2 * g + 2] for g in range(4)], axis=0)
        return first, second

    zero = jnp.zeros((RHS, 128), F32)

    rhs_copy().wait()

    def load_rhs(e):
        v = twice(rhs_in[place[e]])
        r0[e] = v
        split(packed_w, e, v)

    loop(0, ROWS, load_rhs, 16)
    pl.semaphore_wait(barrier, greeted)
    send_top(0, r0)

    def gz_copy():
        return pltpu.make_async_remote_copy(src_ref=gz_send, dst_ref=gz_recv, send_sem=gz_ssem, recv_sem=gz_rsem,
                                            device_id=(below,), device_id_type=MESH)

    def g0_copy():
        return pltpu.make_async_remote_copy(src_ref=g0_send, dst_ref=g0_recv, send_sem=g0_ssem, recv_sem=g0_rsem,
                                            device_id=(below,), device_id_type=MESH)

    def fill_gz(j):
        gz_send[j] = jnp.concatenate([g_in[place[2 * j], 3], g_in[place[2 * j + 1], 3]], axis=1)

    def fill_g0(j):
        pair = [g_in[place[(2 * j + s) // 3], (2 * j + s) % 3] for s in range(2)]
        g0_send[j] = jnp.concatenate(pair, axis=1)

    def split_pairs(received, ref, pairs):
        def one(j):
            v = received[j]
            ref[2 * j] = split_block(v[:, :DOFS])
            ref[2 * j + 1] = split_block(v[:, DOFS:])

        loop(0, pairs, one)

    chunks = ROWS // G_CHUNK
    for c in range(chunks):
        g_copy(c).wait()
        if c == chunks - 1:
            loop(0, FACE // 2, fill_gz)
            gz_copy().start()
        convert_g(c)

    def first_side():
        loop(0, FACE * 3 // 2, fill_g0)
        g0_copy().start()
        for c in range(ROWS // A_CHUNK - 2):
            convert_a(c)
        gz_copy().wait_recv()
        split_pairs(gz_recv, gz_w, FACE // 2)

    def second_side():
        for c in range(ROWS // A_CHUNK - 2, ROWS // A_CHUNK):
            convert_a(c)

    first_product(r0, u0, w0, first_side, second_side)

    def dots0(e, carry):
        split(packed_w, e, w0[e])
        return carry[0] + r0[e] * u0[e], carry[1] + w0[e] * u0[e]

    value = dot_pack(*lax.fori_loop(0, ROWS, dots0, (zero, zero), unroll=16))
    dot_start(0, 0, value)

    def beside1():
        dot_start(0, 1, dot_finish(0, 0))
        g0_copy().wait_recv()
        split_pairs(g0_recv, g0_w, FACE * 3 // 2)

    def beside2():
        dot_start(1, 1, dot_finish(1, 0))

    later_product(1, w0, m0, n0, beside1)
    gam0, del0 = dot_unpack(dot_finish(0, 1))
    alpha0 = gam0 / del0
    al0 = jnp.broadcast_to(alpha0, (RHS, 128))

    def update0(e, carry):
        u = u0[e] - al0 * m0[e]
        w = w0[e] - al0 * n0[e]
        r = r0[e] - al0 * w0[e]
        u1[e] = u
        w1[e] = w
        split(packed_w, e, w)
        return carry[0] + r * u, carry[1] + w * u

    value = dot_pack(*lax.fori_loop(0, ROWS, update0, (zero, zero), unroll=16))
    dot_start(1, 0, value)

    later_product(2, w1, m1, n1, beside2)
    gam1, del1 = dot_unpack(dot_finish(1, 1))
    beta1 = gam1 / gam0
    alpha1 = gam1 / (del1 - beta1 * gam1 / alpha0)
    al1 = jnp.broadcast_to(alpha1, (RHS, 128))
    ab1 = jnp.broadcast_to(alpha1 * beta1, (RHS, 128))
    be1 = jnp.broadcast_to(beta1, (RHS, 128))
    k0 = jnp.broadcast_to(alpha0 + alpha1 * beta1, (RHS, 128))

    def update1(e, carry):
        u = u1[e] - (al1 * m1[e] + ab1 * m0[e])
        w = w1[e] - (al1 * n1[e] + ab1 * n0[e])
        r = r0[e] - (k0 * w0[e] + al1 * w1[e])
        m1[e] = u
        n1[e] = w
        return carry[0] + r * u, carry[1] + w * u

    value = dot_pack(*lax.fori_loop(0, ROWS, update1, (zero, zero), unroll=16))
    dot_start(2, 0, value)

    def prepare(i):
        e = inverse[0, i]
        u, w = u0[e], w0[e]
        v, q = u1[e], w1[e]
        for k, part in enumerate((k0 * u + al1 * v, m1[e], v + be1 * u, r0[e] - (k0 * w + al1 * q), n1[e], q + be1 * w)):
            parts[k, i] = part[:, :DOFS]

    loop(0, ROWS, prepare, 16)
    parts_copy = pltpu.make_async_copy(parts, parts_hbm, out_sem.at[0])
    parts_copy.start()
    dot_start(2, 1, dot_finish(2, 0))
    gam2, del2 = dot_unpack(dot_finish(2, 1))
    beta2 = gam2 / gam1
    alpha2 = gam2 / (del2 - beta2 * gam2 / alpha1)
    coef[0] = jnp.broadcast_to(alpha2, (RHS, DOFS))
    coef[1] = jnp.broadcast_to(alpha2 * beta2, (RHS, DOFS))
    ends = [parts_copy]
    for k, ref in enumerate((alpha_hbm, alpha_beta_hbm)):
        ends.append(pltpu.make_async_copy(coef.at[k], ref, out_sem.at[1 + k]))
        ends[-1].start()
    for c in ends:
        c.wait()

    gz_copy().wait_send()
    g0_copy().wait_send()
    for slot in range(12):
        halo_copy(slot).wait_send()
    for number in range(3):
        for stage in range(2):
            slots = dot_slots(number, stage)
            pltpu.make_async_copy(slots, slots, dot_ssem.at[number, stage]).wait()


def body(right_side, a_blocks, a_cols, g_blocks, g_cols, send_up, send_down):
    field = pltpu.VMEM((ROWS, RHS, 128), F32)
    packed = pltpu.VMEM((ROWS, 2 * RHS, 128), BF16)
    edge = pltpu.VMEM((FACE, RHS, 128), F32)
    face = pltpu.VMEM((FACE, 2 * RHS, 128), BF16)
    hbm = pl.BlockSpec(memory_space=pl.ANY)
    smem = pl.BlockSpec(memory_space=pltpu.SMEM)
    dma = pltpu.SemaphoreType.DMA
    pairs = FACE // 2
    small = jax.ShapeDtypeStruct((RHS, DOFS), F32)
    parts, alpha, alpha_beta = pl.pallas_call(
        kernel,
        out_shape=(jax.ShapeDtypeStruct((6, ROWS, RHS, DOFS), F32), small, small),
        in_specs=[hbm, hbm, hbm, smem, smem, smem],
        out_specs=(hbm, hbm, hbm),
        scratch_shapes=[
            pltpu.VMEM((ROWS, RHS, DOFS), F32),
            pltpu.VMEM((A_SLOTS, A_CHUNK, 7, DOFS, DOFS), F32),
            pltpu.VMEM((ROWS, 4, DOFS, DOFS), F32),
            pltpu.VMEM((ROWS * 7, DOFS, 128), BF16),
            pltpu.VMEM((ROWS * 4, DOFS, 128), BF16),
            pltpu.VMEM((FACE, DOFS, 128), BF16),
            pltpu.VMEM((FACE * 3, DOFS, 128), BF16),
            packed, packed, packed,
            face, face, face, face, face, face,
            edge, edge, edge, edge,
            field, field, field, field, field, field, field, field, field,
            pltpu.VMEM((6, ROWS, RHS, DOFS), F32),
            pltpu.VMEM((2, RHS, DOFS), F32),
            pltpu.VMEM((pairs, DOFS, 128), F32),
            pltpu.VMEM((pairs, DOFS, 128), F32),
            pltpu.VMEM((pairs * 3, DOFS, 128), F32),
            pltpu.VMEM((pairs * 3, DOFS, 128), F32),
            pltpu.VMEM((12, FACE // 2, RHS, 128), F32),
            pltpu.VMEM((12, FACE // 2, RHS, 128), F32),
            pltpu.VMEM((3, 2, 8, 128), F32),
            pltpu.VMEM((3, FIRST_SLOT[2], 8, 128), F32),
            pltpu.SMEM((ROWS,), jnp.int32),
            pltpu.SMEM((8, 128), jnp.int32),
            pltpu.SMEM((ROWS * 4,), jnp.int32),
            pltpu.SMEM((FACE,), jnp.int32),
            pltpu.SMEM((FACE,), jnp.int32),
            pltpu.SMEM((2 * FACE,), jnp.int32),
            pltpu.SMEM((2 * FACE,), jnp.int32),
            pltpu.VMEM((8, 128), jnp.int32),
            dma((5,)), dma((A_SLOTS,)), dma((3,)), dma, dma, dma, dma, dma,
            dma((12,)), dma((12,)), dma((3, 2)), dma((3, 2)),
        ],
        compiler_params=pltpu.CompilerParams(
            collective_id=0, has_side_effects=True, vmem_limit_bytes=60 * 2 ** 20),
    )(right_side, a_blocks, g_blocks, a_cols.T, send_up, send_down)
    return (parts[0] + (alpha * parts[1] + alpha_beta * parts[2]),
            parts[3] - (alpha * parts[4] + alpha_beta * parts[5]))


def solution(mesh):
    in_specs = (
        P("dom", None, None),
        P("dom", None, None, None),
        P("dom", None),
        P("dom", None, None, None),
        P("dom", None),
        P("dom", None),
        P("dom", None),
    )
    out_specs = (P("dom", None, None), P("dom", None, None))
    return jax.shard_map(body, mesh=mesh, in_specs=in_specs, out_specs=out_specs, check_vma=False)
```

```python
import itertools

import jax
import jax.numpy as jnp
from jax import lax
from jax.experimental import pallas as pl
from jax.experimental.pallas import tpu as pltpu
from jax.sharding import PartitionSpec as P

ROWS = 64
FACE = 16
LAYERS = 4
RHS = 32
DOFS = 64
MESH = pl.DeviceIdType.MESH
NT = (((1,), (1,)), ((), ()))
F32 = jnp.float32
BF16 = jnp.bfloat16
G_CHUNK = 16
A_CHUNK = 8
A_SLOTS = 4
GROUPS = (((1, 2), (2, 4), (64, 4)), ((8, 8),))
FIRST_SLOT = (0, 31, 38)
LAST_CHUNKS = 4


def loop(lo, hi, fn, unroll=None):
    def step(i, carry):
        fn(i)
        return carry

    lax.fori_loop(lo, hi, step, 0, unroll=(hi - lo) if unroll is None else unroll)


def kernel(rhs_hbm, a_hbm, g_hbm, cols, send_up, send_down, parts_hbm, coef_hbm,
           rhs_in, a_in, g_in, a_w, g_w, gz_w, g0_w, packed_w, packed_y, packed_m,
           low_w, high_y, low_m, high_m, y_loc, y_far, u_low, u_high,
           r0, u0, w0, m0, n0, u1, w1, m1, n1, parts, coef,
           gz_send, gz_recv, g0_send, g0_recv, halo_send, halo_recv, dot_send, dot_recv,
           place, inverse, near, low_at, high_at, high_side, inverse_vec,
           in_sem, a_sem, out_sem, tab_sem, gz_ssem, gz_rsem, g0_ssem, g0_rsem, halo_ssem, halo_rsem, dot_ssem, dot_rsem):
    count = lax.axis_size("dom")
    me = lax.axis_index("dom")
    above = lax.rem(me + 1, count)
    below = lax.rem(me + count - 1, count)

    def partners(stage):
        out = []
        for steps in itertools.product(*[range(size) for _, size in GROUPS[stage]]):
            device = me
            for (stride, size), step in zip(GROUPS[stage], steps):
                if step:
                    mine = lax.rem(me // stride, size)
                    device = device + (lax.rem(mine + step, size) - mine) * stride
            if any(steps):
                out.append(device)
        return out

    def rhs_copy():
        return pltpu.make_async_copy(rhs_hbm, rhs_in, in_sem.at[0])

    def g_copy(c):
        part = pl.ds(c * G_CHUNK, G_CHUNK)
        return pltpu.make_async_copy(g_hbm.at[part], g_in.at[part], in_sem.at[1 + c])

    def a_copy(c):
        return pltpu.make_async_copy(a_hbm.at[pl.ds(c * A_CHUNK, A_CHUNK)], a_in.at[c % A_SLOTS], a_sem.at[c % A_SLOTS])

    rhs_copy().start()
    for c in range(ROWS // G_CHUNK):
        g_copy(c).start()
    for c in range(A_SLOTS):
        a_copy(c).start()

    barrier = pltpu.get_barrier_semaphore()
    greeted = 2
    for device in (above, below):
        pl.semaphore_signal(barrier, inc=1, device_id=(device,), device_id_type=MESH)
    for stage in range(2):
        for device in partners(stage):
            pl.semaphore_signal(barrier, inc=1, device_id=(device,), device_id_type=MESH)
            greeted += 1

    def first_layer(h):
        place[h] = send_down[0, h]

    loop(0, FACE, first_layer)

    def next_layer(e):
        place[e + FACE] = cols[5, place[e]]

    loop(0, ROWS - FACE, next_layer, 1)
    tab_lane = lax.broadcasted_iota(jnp.int32, (8, 128), 1)
    vec = lax.fori_loop(0, ROWS, lambda e, v: jnp.where(tab_lane == place[e], e, v),
                        jnp.zeros((8, 128), jnp.int32), unroll=8)
    inverse_vec[...] = vec
    tab = pltpu.make_async_copy(inverse_vec, inverse, tab_sem)
    tab.start()
    tab.wait()

    def neighbours(e):
        row = place[e]
        for k in range(4):
            near[e * 4 + k] = inverse[0, cols[k, row]]

    loop(0, ROWS, neighbours, 4)

    def crossings(h):
        low_at[h] = jnp.clip(cols[4, place[h]] - ROWS, 0, FACE - 1)
        high_at[h] = jnp.clip(cols[5, place[3 * FACE + h]] - (ROWS + FACE), 0, FACE - 1)

        for s in range(2):
            high_side[h * 2 + s] = jnp.clip(near[(3 * FACE + h) * 4 + 1 + 2 * s] - 3 * FACE, 0, FACE - 1)

    loop(0, FACE, crossings, 4)

    left = lax.broadcasted_iota(jnp.int32, (RHS, 128), 1) < DOFS
    left2 = lax.broadcasted_iota(jnp.int32, (2 * RHS, 128), 1) < DOFS

    def twice(v):
        return jnp.concatenate([v, v], axis=1)

    def split(ref, e, v):
        hi = v.astype(BF16)
        ref[e, 0:RHS] = hi
        ref[e, RHS:2 * RHS] = (v - hi.astype(F32)).astype(BF16)

    def split_block(v):
        hi = v.astype(BF16)
        lo = (v - hi.astype(F32)).astype(BF16)
        return jnp.concatenate([hi, lo], axis=1)

    def times(fields, weights):
        out = lax.dot_general(jnp.concatenate(fields, axis=1), jnp.concatenate(weights, axis=1), NT,
                              preferred_element_type=F32)
        return out[:RHS] + out[RHS:]

    def times_transposed(fields, weights):
        pair = [jnp.where(left2, fields[i], fields[i + 1]) for i in range(0, len(fields) - 1, 2)]
        if len(fields) % 2:
            pair.append(fields[-1][:, :DOFS])
        out = jnp.dot(jnp.concatenate(pair, axis=1), jnp.concatenate(weights, axis=0), preferred_element_type=F32)
        out = out[:RHS] + out[RHS:]
        return out + pltpu.roll(out, DOFS, 1)

    def convert_g(c):
        def one(b):
            i = c * G_CHUNK + b // 4
            k = b % 4
            g_w[i * 4 + k] = split_block(g_in[i, k])

        loop(0, G_CHUNK * 4, one)

    def convert_a(c):
        a_copy(c).wait()
        slot = c % A_SLOTS

        def one(i):
            for k in range(7):
                a_w[(c * A_CHUNK + i) * 7 + k] = split_block(a_in[slot, i, k])

        loop(0, A_CHUNK, one)
        if c + A_SLOTS < ROWS // A_CHUNK:
            a_copy(c + A_SLOTS).start()

    def halo_copy(slot):
        return pltpu.make_async_remote_copy(
            src_ref=halo_send.at[slot], dst_ref=halo_recv.at[slot], send_sem=halo_ssem.at[slot],
            recv_sem=halo_rsem.at[slot], device_id=(above if slot % 2 == 0 else below,), device_id_type=MESH)

    def send_top(slot, field):
        def one(j):
            halo_send[slot, j] = jnp.where(left, field[inverse[0, send_up[0, 2 * j]]],
                                           field[inverse[0, send_up[0, 2 * j + 1]]])

        loop(0, FACE // 2, one)
        halo_copy(slot).start()

    def send_bottom(slot, field):
        def one(j):
            halo_send[slot, j] = jnp.where(left, field[2 * j], field[2 * j + 1])

        loop(0, FACE // 2, one)
        halo_copy(slot).start()

    def halves(v):
        turned = pltpu.roll(v, DOFS, 1)
        return jnp.where(left, v, turned), jnp.where(left, turned, v)

    def unpack(slot, ref):
        def one(j):
            ref[2 * j], ref[2 * j + 1] = halves(halo_recv[slot, j])

        loop(0, FACE // 2, one)

    def unpack_split(slot, ref):
        def one(j):
            first, second = halves(halo_recv[slot, j])
            split(ref, 2 * j, first)
            split(ref, 2 * j + 1, second)

        loop(0, FACE // 2, one)

    def row_y(e, below_block):
        row = place[e] * 4
        return times([packed_w[e], packed_w[near[e * 4]], packed_w[near[e * 4 + 2]], below_block],
                     [g_w[row], g_w[row + 1], g_w[row + 2], g_w[row + 3]])

    def row_u(e, above_block, above_weight):
        ex = near[e * 4 + 1]
        ey = near[e * 4 + 3]
        return times_transposed(
            [packed_y[e], packed_y[ex], packed_y[ey], above_block],
            [g_w[place[e] * 4], g_w[place[ex] * 4 + 1], g_w[place[ey] * 4 + 2], above_weight])

    def row_a(e, below_block, above_block):
        row = place[e] * 7
        return twice(times(
            [packed_m[e]] + [packed_m[near[e * 4 + k]] for k in range(4)] + [below_block, above_block],
            [a_w[row + k] for k in range(7)]))

    def bottom(h):
        row = place[h] * 4
        y_loc[h] = twice(times([packed_w[h], packed_w[near[h * 4]], packed_w[near[h * 4 + 2]]],
                               [g_w[row], g_w[row + 1], g_w[row + 2]]))

    def inner_y(e):
        split(packed_y, e, twice(row_y(e, packed_w[e - FACE])))

    def first_product(out_m, out_n, beside_first, beside_inner, beside_second):
        loop(0, FACE, bottom)
        send_bottom(1, y_loc)
        beside_first()
        loop(FACE, ROWS, inner_y)

        def put_u(e, v):
            out_m[e] = v
            split(packed_m, e, v)

        def inner_u(e):
            put_u(e, row_u(e, packed_y[e + FACE], g_w[place[e + FACE] * 4 + 3]))

        loop(FACE, 3 * FACE, inner_u)
        beside_inner()
        halo_copy(0).wait_recv()
        halo_copy(1).wait_recv()
        unpack_split(0, low_w)
        unpack(1, y_far)

        def close_y(h):
            extra = times([low_w[low_at[h]]], [g_w[place[h] * 4 + 3]])
            split(packed_y, h, y_loc[h] + twice(extra))
            t = high_at[h]
            more = times([packed_w[3 * FACE + h]], [gz_w[t]])
            split(high_y, h, y_far[t] + twice(more))

        loop(0, FACE, close_y)

        def outer_u(h):
            put_u(h, row_u(h, packed_y[h + FACE], g_w[place[h + FACE] * 4 + 3]))
            e = 3 * FACE + h
            put_u(e, row_u(e, high_y[h], gz_w[high_at[h]]))

        loop(0, FACE, outer_u)
        send_bottom(3, out_m)
        send_top(2, out_m)
        beside_second()

        def inner_a(e):
            out_n[e] = row_a(e, packed_m[e - FACE], packed_m[e + FACE])

        loop(FACE, 3 * FACE, inner_a)
        halo_copy(2).wait_recv()
        halo_copy(3).wait_recv()
        unpack_split(2, low_m)
        unpack_split(3, high_m)

        def outer_a(h):
            out_n[h] = row_a(h, low_m[low_at[h]], packed_m[h + FACE])
            e = 3 * FACE + h
            out_n[e] = row_a(e, packed_m[e - FACE], high_m[high_at[h]])

        loop(0, FACE, outer_a)

    def later_product(number, out_m, out_n, beside):
        base = number * 4

        def part_high(h):
            e = 3 * FACE + h
            ex = near[e * 4 + 1]
            ey = near[e * 4 + 3]
            out_m[e] = times_transposed([packed_y[e], packed_y[ex], packed_y[ey]],
                                        [g_w[place[e] * 4], g_w[place[ex] * 4 + 1], g_w[place[ey] * 4 + 2]])

        def part_low(h):
            out_m[h] = times_transposed([packed_y[h + FACE]], [g_w[place[h + FACE] * 4 + 3]])

        loop(3 * FACE, ROWS, inner_y)
        loop(0, FACE, part_high)
        send_top(base + 2, out_m)
        loop(0, FACE, bottom)
        send_bottom(base + 1, y_loc)
        loop(FACE, 2 * FACE, inner_y)
        loop(0, FACE, part_low)
        send_bottom(base + 3, out_m)
        loop(2 * FACE, 3 * FACE, inner_y)

        def put_u(e, v):
            out_m[e] = v
            split(packed_m, e, v)

        def inner_u(e):
            put_u(e, row_u(e, packed_y[e + FACE], g_w[place[e + FACE] * 4 + 3]))

        loop(FACE, 3 * FACE, inner_u)

        def part_a(h):
            for layer, k, other in ((1, 6, 2), (2, 5, 1)):
                e = layer * FACE + h
                row = place[e] * 7
                out_n[e] = twice(times(
                    [packed_m[e]] + [packed_m[near[e * 4 + i]] for i in range(4)] + [packed_m[other * FACE + h]],
                    [a_w[row + i] for i in range(5)] + [a_w[row + k]]))

        loop(0, FACE, part_a)
        beside()

        halo_copy(base).wait_recv()
        unpack_split(base, low_w)
        halo_copy(base + 2).wait_recv()
        unpack(base + 2, u_low)

        def close_y_low(h):
            extra = twice(times([low_w[low_at[h]]], [g_w[place[h] * 4 + 3]]))
            split(packed_y, h, y_loc[h] + extra)

        def close_u_low(h):
            ex, ey = near[h * 4 + 1], near[h * 4 + 3]
            put_u(h, out_m[h] + times_transposed(
                [packed_y[h], packed_y[ex], packed_y[ey]],
                [g_w[place[h] * 4], g_w[place[ex] * 4 + 1], g_w[place[ey] * 4 + 2]]))
            split(low_m, h, u_low[low_at[h]] + times_transposed([packed_y[h]], [g_w[place[h] * 4 + 3]]))

        def close_a_low(h):
            out_n[h] = row_a(h, low_m[h], packed_m[h + FACE])
            e = FACE + h
            out_n[e] = out_n[e] + twice(times([packed_m[h]], [a_w[place[e] * 7 + 5]]))

        loop(0, FACE, close_y_low)
        loop(0, FACE, close_u_low)
        loop(0, FACE, close_a_low)

        halo_copy(base + 1).wait_recv()
        halo_copy(base + 3).wait_recv()
        unpack(base + 1, y_far)
        unpack(base + 3, u_high)

        def close_y_high(h):
            more = twice(times([packed_w[3 * FACE + h]], [gz_w[high_at[h]]]))
            split(high_y, h, y_far[high_at[h]] + more)

        def close_u_high(h):
            e = 3 * FACE + h
            put_u(e, out_m[e] + times_transposed([high_y[h]], [gz_w[high_at[h]]]))
            hx, hy = high_side[2 * h], high_side[2 * h + 1]
            split(high_m, h, u_high[high_at[h]] + times_transposed(
                [high_y[h], high_y[hx], high_y[hy]],
                [g0_w[high_at[h] * 3], g0_w[high_at[hx] * 3 + 1], g0_w[high_at[hy] * 3 + 2]]))

        def close_a_high(h):
            e = 3 * FACE + h
            out_n[e] = row_a(e, packed_m[e - FACE], high_m[h])
            e = 2 * FACE + h
            out_n[e] = out_n[e] + twice(times([packed_m[e + FACE]], [a_w[place[e] * 7 + 6]]))

        loop(0, FACE, close_y_high)
        loop(0, FACE, close_u_high)
        loop(0, FACE, close_a_high)

    dot_lane = lax.broadcasted_iota(jnp.int32, (RHS, 128), 1)
    dot_row = lax.broadcasted_iota(jnp.int32, (RHS, 128), 0)

    def dot_slots(number, stage):
        return dot_recv.at[number, pl.ds(FIRST_SLOT[stage], FIRST_SLOT[stage + 1] - FIRST_SLOT[stage])]

    def dot_start(number, stage, value):
        dot_send[number, stage] = value
        for i, device in enumerate(partners(stage)):
            pltpu.make_async_remote_copy(
                src_ref=dot_send.at[number, stage], dst_ref=dot_recv.at[number, FIRST_SLOT[stage] + i],
                send_sem=dot_ssem.at[number, stage], recv_sem=dot_rsem.at[number, stage],
                device_id=(device,), device_id_type=MESH).start()

    def dot_finish(number, stage):
        slots = dot_slots(number, stage)
        pltpu.make_async_copy(slots, slots, dot_rsem.at[number, stage]).wait()
        got = dot_recv[number, FIRST_SLOT[stage]:FIRST_SLOT[stage + 1]]
        return dot_send[number, stage] + jnp.sum(got, axis=0)

    def dot_pack(first, second):
        first = jnp.sum(first, axis=1, keepdims=True)
        second = jnp.sum(second, axis=1, keepdims=True)
        spread = jnp.where(dot_lane == dot_row, first, jnp.where(dot_lane == dot_row + RHS, second, 0.0))
        return jnp.sum(spread, axis=0, keepdims=True)

    def dot_unpack(v):
        first = jnp.sum(jnp.where(dot_lane == dot_row, v, 0.0), axis=1, keepdims=True)
        second = jnp.sum(jnp.where(dot_lane == dot_row + RHS, v, 0.0), axis=1, keepdims=True)
        return first, second

    zero = jnp.zeros((RHS, 128), F32)

    rhs_copy().wait()

    def load_rhs(e):
        v = twice(rhs_in[place[e]])
        r0[e] = v
        split(packed_w, e, v)

    loop(0, ROWS, load_rhs, 16)
    pl.semaphore_wait(barrier, greeted)
    send_top(0, r0)

    def gz_copy():
        return pltpu.make_async_remote_copy(src_ref=gz_send, dst_ref=gz_recv, send_sem=gz_ssem, recv_sem=gz_rsem,
                                            device_id=(below,), device_id_type=MESH)

    def g0_copy():
        return pltpu.make_async_remote_copy(src_ref=g0_send, dst_ref=g0_recv, send_sem=g0_ssem, recv_sem=g0_rsem,
                                            device_id=(below,), device_id_type=MESH)

    def fill_gz(j):
        gz_send[j] = jnp.concatenate([g_in[place[2 * j], 3], g_in[place[2 * j + 1], 3]], axis=1)

    def fill_g0(j):
        pair = [g_in[place[(2 * j + s) // 3], (2 * j + s) % 3] for s in range(2)]
        g0_send[j] = jnp.concatenate(pair, axis=1)

    def split_pairs(received, ref, pairs):
        def one(j):
            v = received[j]
            ref[2 * j] = split_block(v[:, :DOFS])
            ref[2 * j + 1] = split_block(v[:, DOFS:])

        loop(0, pairs, one)

    chunks = ROWS // G_CHUNK
    for c in range(chunks):
        g_copy(c).wait()
        if c == chunks - 1:
            loop(0, FACE // 2, fill_gz)
            gz_copy().start()
        convert_g(c)

    def first_side():
        loop(0, FACE * 3 // 2, fill_g0)
        for c in range(ROWS // A_CHUNK - 2):
            convert_a(c)

    def inner_side():
        halo_copy(1).wait_send()
        gz_copy().wait_send()
        g0_copy().start()
        gz_copy().wait_recv()
        split_pairs(gz_recv, gz_w, FACE // 2)

    def second_side():
        for c in range(ROWS // A_CHUNK - 2, ROWS // A_CHUNK):
            convert_a(c)

    first_product(u0, w0, first_side, inner_side, second_side)
    send_top(4, w0)

    def dots0(e, carry):
        split(packed_w, e, w0[e])
        return carry[0] + r0[e] * u0[e], carry[1] + w0[e] * u0[e]

    value = dot_pack(*lax.fori_loop(0, ROWS, dots0, (zero, zero), unroll=16))
    dot_start(0, 0, value)

    def beside1():
        dot_start(0, 1, dot_finish(0, 0))
        g0_copy().wait_recv()
        split_pairs(g0_recv, g0_w, FACE * 3 // 2)

    def beside2():
        dot_start(1, 1, dot_finish(1, 0))

    later_product(1, m0, n0, beside1)
    gam0, del0 = dot_unpack(dot_finish(0, 1))
    alpha0 = gam0 / del0
    al0 = jnp.broadcast_to(alpha0, (RHS, 128))

    def update0(e, carry):
        u = u0[e] - al0 * m0[e]
        w = w0[e] - al0 * n0[e]
        r = r0[e] - al0 * w0[e]
        u1[e] = u
        w1[e] = w
        split(packed_w, e, w)
        return carry[0] + r * u, carry[1] + w * u

    sums = lax.fori_loop(3 * FACE, ROWS, update0, (zero, zero), unroll=16)
    send_top(8, w1)
    dot_start(1, 0, dot_pack(*lax.fori_loop(0, 3 * FACE, update0, sums, unroll=16)))

    later_product(2, m1, n1, beside2)
    gam1, del1 = dot_unpack(dot_finish(1, 1))
    beta1 = gam1 / gam0
    alpha1 = gam1 / (del1 - beta1 * gam1 / alpha0)
    al1 = jnp.broadcast_to(alpha1, (RHS, 128))
    ab1 = jnp.broadcast_to(alpha1 * beta1, (RHS, 128))
    be1 = jnp.broadcast_to(beta1, (RHS, 128))
    k0 = jnp.broadcast_to(alpha0 + alpha1 * beta1, (RHS, 128))

    def update1(e, carry):
        u = u1[e] - (al1 * m1[e] + ab1 * m0[e])
        w = w1[e] - (al1 * n1[e] + ab1 * n0[e])
        r = r0[e] - (k0 * w0[e] + al1 * w1[e])
        m1[e] = u
        n1[e] = w
        return carry[0] + r * u, carry[1] + w * u

    value = dot_pack(*lax.fori_loop(0, ROWS, update1, (zero, zero), unroll=16))
    dot_start(2, 0, value)

    def prepare(e):
        u, w = u0[e], w0[e]
        v, q = u1[e], w1[e]
        return k0 * u + al1 * v, m1[e], v + be1 * u, r0[e] - (k0 * w + al1 * q), n1[e], q + be1 * w

    def prepare_pair(j):
        for k, (a, b) in enumerate(zip(prepare(inverse[0, 2 * j]), prepare(inverse[0, 2 * j + 1]))):
            parts[k, j] = jnp.where(left, a, b)

    loop(0, ROWS // 2, prepare_pair, 8)
    parts_copy = pltpu.make_async_copy(parts, parts_hbm, out_sem.at[0])
    parts_copy.start()
    dot_start(2, 1, dot_finish(2, 0))
    gam2, del2 = dot_unpack(dot_finish(2, 1))
    beta2 = gam2 / gam1
    alpha2 = gam2 / (del2 - beta2 * gam2 / alpha1)
    coef[0] = jnp.broadcast_to(alpha2, (RHS, 128))
    coef[1] = jnp.broadcast_to(alpha2 * beta2, (RHS, 128))
    coef_copy = pltpu.make_async_copy(coef, coef_hbm, out_sem.at[1])
    coef_copy.start()
    parts_copy.wait()
    coef_copy.wait()

    g0_copy().wait_send()
    for slot in range(12):
        if slot != 1:
            halo_copy(slot).wait_send()
    for number in range(3):
        for stage in range(2):
            slots = dot_slots(number, stage)
            pltpu.make_async_copy(slots, slots, dot_ssem.at[number, stage]).wait()


def finish(parts_hbm, coef_hbm, x_hbm, r_hbm, parts, coef, x_out, r_out, in_sem, coef_sem, out_sem):
    size = ROWS // 2 // LAST_CHUNKS
    coef_copy = pltpu.make_async_copy(coef_hbm, coef, coef_sem)
    coef_copy.start()
    copies = []
    for c in range(LAST_CHUNKS):
        part = pl.ds(c * size, size)
        copies.append(pltpu.make_async_copy(parts_hbm.at[:, part], parts.at[:, part], in_sem.at[c]))
        copies[-1].start()
    coef_copy.wait()
    alpha, alpha_beta = coef[0], coef[1]
    ends = []
    for c in range(LAST_CHUNKS):
        copies[c].wait()

        def one(j):
            x = parts[0, j] + (alpha * parts[1, j] + alpha_beta * parts[2, j])
            r = parts[3, j] - (alpha * parts[4, j] + alpha_beta * parts[5, j])
            for ref, v in ((x_out, x), (r_out, r)):
                ref[2 * j] = v[:, :DOFS]
                ref[2 * j + 1] = v[:, DOFS:]

        loop(c * size, (c + 1) * size, one)
        rows = pl.ds(2 * c * size, 2 * size)
        for k, (ref, hbm) in enumerate(((x_out, x_hbm), (r_out, r_hbm))):
            ends.append(pltpu.make_async_copy(ref.at[rows], hbm.at[rows], out_sem.at[k, c]))
            ends[-1].start()
    for c in ends:
        c.wait()


def body(right_side, a_blocks, a_cols, g_blocks, g_cols, send_up, send_down):
    field = pltpu.VMEM((ROWS, RHS, 128), F32)
    packed = pltpu.VMEM((ROWS, 2 * RHS, 128), BF16)
    edge = pltpu.VMEM((FACE, RHS, 128), F32)
    face = pltpu.VMEM((FACE, 2 * RHS, 128), BF16)
    hbm = pl.BlockSpec(memory_space=pl.ANY)
    smem = pl.BlockSpec(memory_space=pltpu.SMEM)
    dma = pltpu.SemaphoreType.DMA
    pairs = FACE // 2
    parts, coef = pl.pallas_call(
        kernel,
        out_shape=(jax.ShapeDtypeStruct((6, ROWS // 2, RHS, 128), F32), jax.ShapeDtypeStruct((2, RHS, 128), F32)),
        in_specs=[hbm, hbm, hbm, smem, smem, smem],
        out_specs=(hbm, hbm),
        scratch_shapes=[
            pltpu.VMEM((ROWS, RHS, DOFS), F32),
            pltpu.VMEM((A_SLOTS, A_CHUNK, 7, DOFS, DOFS), F32),
            pltpu.VMEM((ROWS, 4, DOFS, DOFS), F32),
            pltpu.VMEM((ROWS * 7, DOFS, 128), BF16),
            pltpu.VMEM((ROWS * 4, DOFS, 128), BF16),
            pltpu.VMEM((FACE, DOFS, 128), BF16),
            pltpu.VMEM((FACE * 3, DOFS, 128), BF16),
            packed, packed, packed,
            face, face, face, face,
            edge, edge, edge, edge,
            field, field, field, field, field, field, field, field, field,
            pltpu.VMEM((6, ROWS // 2, RHS, 128), F32),
            pltpu.VMEM((2, RHS, 128), F32),
            pltpu.VMEM((pairs, DOFS, 128), F32),
            pltpu.VMEM((pairs, DOFS, 128), F32),
            pltpu.VMEM((pairs * 3, DOFS, 128), F32),
            pltpu.VMEM((pairs * 3, DOFS, 128), F32),
            pltpu.VMEM((12, FACE // 2, RHS, 128), F32),
            pltpu.VMEM((12, FACE // 2, RHS, 128), F32),
            pltpu.VMEM((3, 2, 1, 128), F32),
            pltpu.VMEM((3, FIRST_SLOT[2], 1, 128), F32),
            pltpu.SMEM((ROWS,), jnp.int32),
            pltpu.SMEM((8, 128), jnp.int32),
            pltpu.SMEM((ROWS * 4,), jnp.int32),
            pltpu.SMEM((FACE,), jnp.int32),
            pltpu.SMEM((FACE,), jnp.int32),
            pltpu.SMEM((2 * FACE,), jnp.int32),
            pltpu.VMEM((8, 128), jnp.int32),
            dma((5,)), dma((A_SLOTS,)), dma((2,)), dma, dma, dma, dma, dma,
            dma((12,)), dma((12,)), dma((3, 2)), dma((3, 2)),
        ],
        compiler_params=pltpu.CompilerParams(
            collective_id=0, has_side_effects=True, vmem_limit_bytes=60 * 2 ** 20),
    )(right_side, a_blocks, g_blocks, a_cols.T, send_up, send_down)
    out = jax.ShapeDtypeStruct((ROWS, RHS, DOFS), F32)
    return pl.pallas_call(
        finish,
        out_shape=(out, out),
        in_specs=[hbm, hbm],
        out_specs=(hbm, hbm),
        scratch_shapes=[
            pltpu.VMEM((6, ROWS // 2, RHS, 128), F32),
            pltpu.VMEM((2, RHS, 128), F32),
            pltpu.VMEM((ROWS, RHS, DOFS), F32),
            pltpu.VMEM((ROWS, RHS, DOFS), F32),
            dma((LAST_CHUNKS,)), dma, dma((2, LAST_CHUNKS)),
        ],
        compiler_params=pltpu.CompilerParams(vmem_limit_bytes=60 * 2 ** 20),
    )(parts, coef)


def solution(mesh):
    in_specs = (
        P("dom", None, None),
        P("dom", None, None, None),
        P("dom", None),
        P("dom", None, None, None),
        P("dom", None),
        P("dom", None),
        P("dom", None),
    )
    out_specs = (P("dom", None, None), P("dom", None, None))
    return jax.shard_map(body, mesh=mesh, in_specs=in_specs, out_specs=out_specs, check_vma=False)
```

```python
import itertools

import jax
import jax.numpy as jnp
from jax import lax
from jax.experimental import pallas as pl
from jax.experimental.pallas import tpu as pltpu
from jax.sharding import PartitionSpec as P

ROWS = 64
FACE = 16
LAYERS = 4
RHS = 32
DOFS = 64
MESH = pl.DeviceIdType.MESH
NT = (((1,), (1,)), ((), ()))
F32 = jnp.float32
BF16 = jnp.bfloat16
G_CHUNK = 16
A_CHUNK = 8
A_SLOTS = 4
GROUPS = (((1, 2), (2, 4), (64, 4)), ((8, 8),))
FIRST_SLOT = (0, 31, 38)
LAST_CHUNKS = 4


def loop(lo, hi, fn, unroll=None):
    def step(i, carry):
        fn(i)
        return carry

    lax.fori_loop(lo, hi, step, 0, unroll=(hi - lo) if unroll is None else unroll)


def kernel(rhs_hbm, a_hbm, g_hbm, cols, send_up, send_down, parts_hbm, coef_hbm,
           rhs_in, a_in, g_in, a_w, g_w, gz_w, g0_w, packed_w, packed_y, packed_m,
           low_w, high_y, low_m, high_m, y_loc, y_far, u_low, u_high,
           r0, u0, w0, m0, n0, u1, w1, m1, n1, parts, coef,
           gz_send, gz_recv, g0_send, g0_recv, halo_send, halo_recv, dot_send, dot_recv,
           place, inverse, near, low_at, high_at, high_side, inverse_vec,
           in_sem, a_sem, out_sem, tab_sem, gz_ssem, gz_rsem, g0_ssem, g0_rsem, halo_ssem, halo_rsem, dot_ssem, dot_rsem):
    count = lax.axis_size("dom")
    me = lax.axis_index("dom")
    above = lax.rem(me + 1, count)
    below = lax.rem(me + count - 1, count)

    def partners(stage):
        out = []
        for steps in itertools.product(*[range(size) for _, size in GROUPS[stage]]):
            device = me
            for (stride, size), step in zip(GROUPS[stage], steps):
                if step:
                    mine = lax.rem(me // stride, size)
                    device = device + (lax.rem(mine + step, size) - mine) * stride
            if any(steps):
                out.append(device)
        return out

    def rhs_copy():
        return pltpu.make_async_copy(rhs_hbm, rhs_in, in_sem.at[0])

    def g_copy(c):
        part = pl.ds(c * G_CHUNK, G_CHUNK)
        return pltpu.make_async_copy(g_hbm.at[part], g_in.at[part], in_sem.at[1 + c])

    def a_copy(c):
        return pltpu.make_async_copy(a_hbm.at[pl.ds(c * A_CHUNK, A_CHUNK)], a_in.at[c % A_SLOTS], a_sem.at[c % A_SLOTS])

    rhs_copy().start()
    for c in range(ROWS // G_CHUNK):
        g_copy(c).start()
    for c in range(A_SLOTS):
        a_copy(c).start()

    barrier = pltpu.get_barrier_semaphore()
    greeted = 2
    for device in (above, below):
        pl.semaphore_signal(barrier, inc=1, device_id=(device,), device_id_type=MESH)
    for stage in range(2):
        for device in partners(stage):
            pl.semaphore_signal(barrier, inc=1, device_id=(device,), device_id_type=MESH)
            greeted += 1

    def first_layer(h):
        place[h] = send_down[0, h]

    loop(0, FACE, first_layer)

    def next_layer(e):
        place[e + FACE] = cols[5, place[e]]

    loop(0, ROWS - FACE, next_layer, 1)
    tab_lane = lax.broadcasted_iota(jnp.int32, (8, 128), 1)
    vec = lax.fori_loop(0, ROWS, lambda e, v: jnp.where(tab_lane == place[e], e, v),
                        jnp.zeros((8, 128), jnp.int32), unroll=8)
    inverse_vec[...] = vec
    tab = pltpu.make_async_copy(inverse_vec, inverse, tab_sem)
    tab.start()
    tab.wait()

    def neighbours(e):
        row = place[e]
        for k in range(4):
            near[e * 4 + k] = inverse[0, cols[k, row]]

    loop(0, ROWS, neighbours, 4)

    def crossings(h):
        low_at[h] = jnp.clip(cols[4, place[h]] - ROWS, 0, FACE - 1)
        high_at[h] = jnp.clip(cols[5, place[3 * FACE + h]] - (ROWS + FACE), 0, FACE - 1)

        for s in range(2):
            high_side[h * 2 + s] = jnp.clip(near[(3 * FACE + h) * 4 + 1 + 2 * s] - 3 * FACE, 0, FACE - 1)

    loop(0, FACE, crossings, 4)

    left = lax.broadcasted_iota(jnp.int32, (RHS, 128), 1) < DOFS
    left2 = lax.broadcasted_iota(jnp.int32, (2 * RHS, 128), 1) < DOFS

    def twice(v):
        return jnp.concatenate([v, v], axis=1)

    def split(ref, e, v):
        hi = v.astype(BF16)
        ref[e, 0:RHS] = hi
        ref[e, RHS:2 * RHS] = (v - hi.astype(F32)).astype(BF16)

    def split_block(v):
        hi = v.astype(BF16)
        lo = (v - hi.astype(F32)).astype(BF16)
        return jnp.concatenate([hi, lo], axis=1)

    def times(fields, weights):
        out = lax.dot_general(jnp.concatenate(fields, axis=1), jnp.concatenate(weights, axis=1), NT,
                              preferred_element_type=F32)
        return out[:RHS] + out[RHS:]

    def times_transposed(fields, weights):
        pair = [jnp.where(left2, fields[i], fields[i + 1]) for i in range(0, len(fields) - 1, 2)]
        if len(fields) % 2:
            pair.append(fields[-1][:, :DOFS])
        out = jnp.dot(jnp.concatenate(pair, axis=1), jnp.concatenate(weights, axis=0), preferred_element_type=F32)
        out = out[:RHS] + out[RHS:]
        return out + pltpu.roll(out, DOFS, 1)

    def convert_g(c):
        def one(b):
            i = c * G_CHUNK + b // 4
            k = b % 4
            g_w[i * 4 + k] = split_block(g_in[i, k])

        loop(0, G_CHUNK * 4, one)

    def convert_a(c):
        a_copy(c).wait()
        slot = c % A_SLOTS

        def one(i):
            for k in range(7):
                a_w[(c * A_CHUNK + i) * 7 + k] = split_block(a_in[slot, i, k])

        loop(0, A_CHUNK, one)
        if c + A_SLOTS < ROWS // A_CHUNK:
            a_copy(c + A_SLOTS).start()

    def halo_copy(slot):
        return pltpu.make_async_remote_copy(
            src_ref=halo_send.at[slot], dst_ref=halo_recv.at[slot], send_sem=halo_ssem.at[slot],
            recv_sem=halo_rsem.at[slot], device_id=(above if slot % 2 == 0 else below,), device_id_type=MESH)

    def send_top(slot, field):
        def one(j):
            halo_send[slot, j] = jnp.where(left, field[inverse[0, send_up[0, 2 * j]]],
                                           field[inverse[0, send_up[0, 2 * j + 1]]])

        loop(0, FACE // 2, one)
        halo_copy(slot).start()

    def send_bottom(slot, field):
        def one(j):
            halo_send[slot, j] = jnp.where(left, field[2 * j], field[2 * j + 1])

        loop(0, FACE // 2, one)
        halo_copy(slot).start()

    def halves(v):
        turned = pltpu.roll(v, DOFS, 1)
        return jnp.where(left, v, turned), jnp.where(left, turned, v)

    def unpack(slot, ref):
        def one(j):
            ref[2 * j], ref[2 * j + 1] = halves(halo_recv[slot, j])

        loop(0, FACE // 2, one)

    def unpack_split(slot, ref):
        def one(j):
            first, second = halves(halo_recv[slot, j])
            split(ref, 2 * j, first)
            split(ref, 2 * j + 1, second)

        loop(0, FACE // 2, one)

    def row_y(e, below_block):
        row = place[e] * 4
        return times([packed_w[e], packed_w[near[e * 4]], packed_w[near[e * 4 + 2]], below_block],
                     [g_w[row], g_w[row + 1], g_w[row + 2], g_w[row + 3]])

    def row_u(e, above_block, above_weight):
        ex = near[e * 4 + 1]
        ey = near[e * 4 + 3]
        return times_transposed(
            [packed_y[e], packed_y[ex], packed_y[ey], above_block],
            [g_w[place[e] * 4], g_w[place[ex] * 4 + 1], g_w[place[ey] * 4 + 2], above_weight])

    def row_a(e, below_block, above_block):
        row = place[e] * 7
        return twice(times(
            [packed_m[e]] + [packed_m[near[e * 4 + k]] for k in range(4)] + [below_block, above_block],
            [a_w[row + k] for k in range(7)]))

    def bottom(h):
        row = place[h] * 4
        y_loc[h] = twice(times([packed_w[h], packed_w[near[h * 4]], packed_w[near[h * 4 + 2]]],
                               [g_w[row], g_w[row + 1], g_w[row + 2]]))

    def inner_y(e):
        split(packed_y, e, twice(row_y(e, packed_w[e - FACE])))

    def first_product(out_m, out_n, beside_first, beside_inner, beside_second):
        loop(0, FACE, bottom)
        send_bottom(1, y_loc)
        beside_first()
        loop(FACE, ROWS, inner_y)

        def put_u(e, v):
            out_m[e] = v
            split(packed_m, e, v)

        def inner_u(e):
            put_u(e, row_u(e, packed_y[e + FACE], g_w[place[e + FACE] * 4 + 3]))

        loop(FACE, 3 * FACE, inner_u)

        halo_copy(0).wait_recv()
        unpack_split(0, low_w)

        def close_y_low(h):
            extra = times([low_w[low_at[h]]], [g_w[place[h] * 4 + 3]])
            split(packed_y, h, y_loc[h] + twice(extra))

        def outer_u_low(h):
            put_u(h, row_u(h, packed_y[h + FACE], g_w[place[h + FACE] * 4 + 3]))

        loop(0, FACE, close_y_low)
        loop(0, FACE, outer_u_low)
        send_bottom(3, out_m)
        beside_inner()
        halo_copy(1).wait_recv()
        unpack(1, y_far)

        def close_y_high(h):
            t = high_at[h]
            more = times([packed_w[3 * FACE + h]], [gz_w[t]])
            split(high_y, h, y_far[t] + twice(more))

        def outer_u_high(h):
            e = 3 * FACE + h
            put_u(e, row_u(e, high_y[h], gz_w[high_at[h]]))

        loop(0, FACE, close_y_high)
        loop(0, FACE, outer_u_high)
        send_top(2, out_m)
        beside_second()

        def inner_a(e):
            out_n[e] = row_a(e, packed_m[e - FACE], packed_m[e + FACE])

        def outer_a_high(h):
            e = 3 * FACE + h
            out_n[e] = row_a(e, packed_m[e - FACE], high_m[high_at[h]])

        def outer_a_low(h):
            out_n[h] = row_a(h, low_m[low_at[h]], packed_m[h + FACE])

        loop(FACE, 3 * FACE, inner_a)
        halo_copy(3).wait_recv()
        unpack_split(3, high_m)
        loop(0, FACE, outer_a_high)
        send_top(4, out_n)
        halo_copy(2).wait_recv()
        unpack_split(2, low_m)
        loop(0, FACE, outer_a_low)

    def later_product(number, out_m, out_n, start_sum, beside, before_high):
        base = number * 4

        def part_high(h):
            e = 3 * FACE + h
            ex = near[e * 4 + 1]
            ey = near[e * 4 + 3]
            out_m[e] = times_transposed([packed_y[e], packed_y[ex], packed_y[ey]],
                                        [g_w[place[e] * 4], g_w[place[ex] * 4 + 1], g_w[place[ey] * 4 + 2]])

        def part_low(h):
            out_m[h] = times_transposed([packed_y[h + FACE]], [g_w[place[h + FACE] * 4 + 3]])

        loop(3 * FACE, ROWS, inner_y)
        loop(0, FACE, part_high)
        send_top(base + 2, out_m)
        start_sum()
        loop(0, FACE, bottom)
        send_bottom(base + 1, y_loc)
        loop(FACE, 2 * FACE, inner_y)
        loop(0, FACE, part_low)
        send_bottom(base + 3, out_m)
        loop(2 * FACE, 3 * FACE, inner_y)

        def put_u(e, v):
            out_m[e] = v
            split(packed_m, e, v)

        def inner_u(e):
            put_u(e, row_u(e, packed_y[e + FACE], g_w[place[e + FACE] * 4 + 3]))

        loop(FACE, 3 * FACE, inner_u)

        def part_a(h):
            for layer, k, other in ((1, 6, 2), (2, 5, 1)):
                e = layer * FACE + h
                row = place[e] * 7
                out_n[e] = twice(times(
                    [packed_m[e]] + [packed_m[near[e * 4 + i]] for i in range(4)] + [packed_m[other * FACE + h]],
                    [a_w[row + i] for i in range(5)] + [a_w[row + k]]))

        loop(0, FACE, part_a)
        beside()

        halo_copy(base).wait_recv()
        unpack_split(base, low_w)
        halo_copy(base + 2).wait_recv()
        unpack(base + 2, u_low)

        def close_y_low(h):
            extra = twice(times([low_w[low_at[h]]], [g_w[place[h] * 4 + 3]]))
            split(packed_y, h, y_loc[h] + extra)

        def close_u_low(h):
            ex, ey = near[h * 4 + 1], near[h * 4 + 3]
            put_u(h, out_m[h] + times_transposed(
                [packed_y[h], packed_y[ex], packed_y[ey]],
                [g_w[place[h] * 4], g_w[place[ex] * 4 + 1], g_w[place[ey] * 4 + 2]]))
            split(low_m, h, u_low[low_at[h]] + times_transposed([packed_y[h]], [g_w[place[h] * 4 + 3]]))

        def close_a_low(h):
            out_n[h] = row_a(h, low_m[h], packed_m[h + FACE])
            e = FACE + h
            out_n[e] = out_n[e] + twice(times([packed_m[h]], [a_w[place[e] * 7 + 5]]))

        loop(0, FACE, close_y_low)
        loop(0, FACE, close_u_low)
        loop(0, FACE, close_a_low)

        before_high()

        halo_copy(base + 1).wait_recv()
        halo_copy(base + 3).wait_recv()
        unpack(base + 1, y_far)
        unpack(base + 3, u_high)

        def close_y_high(h):
            more = twice(times([packed_w[3 * FACE + h]], [gz_w[high_at[h]]]))
            split(high_y, h, y_far[high_at[h]] + more)

        def close_u_high(h):
            e = 3 * FACE + h
            put_u(e, out_m[e] + times_transposed([high_y[h]], [gz_w[high_at[h]]]))
            hx, hy = high_side[2 * h], high_side[2 * h + 1]
            split(high_m, h, u_high[high_at[h]] + times_transposed(
                [high_y[h], high_y[hx], high_y[hy]],
                [g0_w[high_at[h] * 3], g0_w[high_at[hx] * 3 + 1], g0_w[high_at[hy] * 3 + 2]]))

        def close_a_high(h):
            e = 3 * FACE + h
            out_n[e] = row_a(e, packed_m[e - FACE], high_m[h])
            e = 2 * FACE + h
            out_n[e] = out_n[e] + twice(times([packed_m[e + FACE]], [a_w[place[e] * 7 + 6]]))

        loop(0, FACE, close_y_high)
        loop(0, FACE, close_u_high)
        loop(0, FACE, close_a_high)

    dot_lane = lax.broadcasted_iota(jnp.int32, (RHS, 128), 1)
    dot_row = lax.broadcasted_iota(jnp.int32, (RHS, 128), 0)

    def dot_slots(number, stage):
        return dot_recv.at[number, pl.ds(FIRST_SLOT[stage], FIRST_SLOT[stage + 1] - FIRST_SLOT[stage])]

    def dot_start(number, stage, value):
        dot_send[number, stage] = value
        for i, device in enumerate(partners(stage)):
            pltpu.make_async_remote_copy(
                src_ref=dot_send.at[number, stage], dst_ref=dot_recv.at[number, FIRST_SLOT[stage] + i],
                send_sem=dot_ssem.at[number, stage], recv_sem=dot_rsem.at[number, stage],
                device_id=(device,), device_id_type=MESH).start()

    def dot_finish(number, stage):
        slots = dot_slots(number, stage)
        pltpu.make_async_copy(slots, slots, dot_rsem.at[number, stage]).wait()
        got = dot_recv[number, FIRST_SLOT[stage]:FIRST_SLOT[stage + 1]]
        return dot_send[number, stage] + jnp.sum(got, axis=0)

    def dot_pack(first, second):
        first = jnp.sum(first, axis=1, keepdims=True)
        second = jnp.sum(second, axis=1, keepdims=True)
        spread = jnp.where(dot_lane == dot_row, first, jnp.where(dot_lane == dot_row + RHS, second, 0.0))
        return jnp.sum(spread, axis=0, keepdims=True)

    def dot_unpack(v):
        first = jnp.sum(jnp.where(dot_lane == dot_row, v, 0.0), axis=1, keepdims=True)
        second = jnp.sum(jnp.where(dot_lane == dot_row + RHS, v, 0.0), axis=1, keepdims=True)
        return first, second

    zero = jnp.zeros((RHS, 128), F32)

    rhs_copy().wait()

    def load_rhs(e):
        v = twice(rhs_in[place[e]])
        r0[e] = v
        split(packed_w, e, v)

    loop(0, ROWS, load_rhs, 16)
    pl.semaphore_wait(barrier, greeted)
    send_top(0, r0)

    def gz_copy():
        return pltpu.make_async_remote_copy(src_ref=gz_send, dst_ref=gz_recv, send_sem=gz_ssem, recv_sem=gz_rsem,
                                            device_id=(below,), device_id_type=MESH)

    def g0_copy():
        return pltpu.make_async_remote_copy(src_ref=g0_send, dst_ref=g0_recv, send_sem=g0_ssem, recv_sem=g0_rsem,
                                            device_id=(below,), device_id_type=MESH)

    def fill_gz(j):
        gz_send[j] = jnp.concatenate([g_in[place[2 * j], 3], g_in[place[2 * j + 1], 3]], axis=1)

    def fill_g0(j):
        pair = [g_in[place[(2 * j + s) // 3], (2 * j + s) % 3] for s in range(2)]
        g0_send[j] = jnp.concatenate(pair, axis=1)

    def split_pairs(received, ref, pairs):
        def one(j):
            v = received[j]
            ref[2 * j] = split_block(v[:, :DOFS])
            ref[2 * j + 1] = split_block(v[:, DOFS:])

        loop(0, pairs, one)

    chunks = ROWS // G_CHUNK
    for c in range(chunks):
        g_copy(c).wait()
        if c == chunks - 1:
            loop(0, FACE // 2, fill_gz)
            gz_copy().start()
        convert_g(c)

    def first_side():
        loop(0, FACE * 3 // 2, fill_g0)
        for c in range(4):
            convert_a(c)

    def inner_side():
        halo_copy(1).wait_send()
        gz_copy().wait_send()
        g0_copy().start()
        for c in range(4, 6):
            convert_a(c)
        gz_copy().wait_recv()
        split_pairs(gz_recv, gz_w, FACE // 2)

    def second_side():
        for c in range(6, ROWS // A_CHUNK):
            convert_a(c)

    first_product(u0, w0, first_side, inner_side, second_side)

    def dots0(e, carry):
        split(packed_w, e, w0[e])
        return carry[0] + r0[e] * u0[e], carry[1] + w0[e] * u0[e]

    sums0 = lax.fori_loop(0, ROWS, dots0, (zero, zero), unroll=16)

    def beside1():
        dot_start(0, 1, dot_finish(0, 0))

    def background():
        g0_copy().wait_recv()
        split_pairs(g0_recv, g0_w, FACE * 3 // 2)

    def nothing():
        pass

    def beside2():
        dot_start(1, 1, dot_finish(1, 0))

    later_product(1, m0, n0, lambda: dot_start(0, 0, dot_pack(*sums0)), beside1, background)
    gam0, del0 = dot_unpack(dot_finish(0, 1))
    alpha0 = gam0 / del0
    al0 = jnp.broadcast_to(alpha0, (RHS, 128))

    def update0(e, carry):
        u = u0[e] - al0 * m0[e]
        w = w0[e] - al0 * n0[e]
        r = r0[e] - al0 * w0[e]
        u1[e] = u
        w1[e] = w
        split(packed_w, e, w)
        return carry[0] + r * u, carry[1] + w * u

    sums = lax.fori_loop(3 * FACE, ROWS, update0, (zero, zero), unroll=16)
    send_top(8, w1)
    sums1 = lax.fori_loop(0, 3 * FACE, update0, sums, unroll=16)

    later_product(2, m1, n1, lambda: dot_start(1, 0, dot_pack(*sums1)), beside2, nothing)
    gam1, del1 = dot_unpack(dot_finish(1, 1))
    beta1 = gam1 / gam0
    alpha1 = gam1 / (del1 - beta1 * gam1 / alpha0)
    al1 = jnp.broadcast_to(alpha1, (RHS, 128))
    ab1 = jnp.broadcast_to(alpha1 * beta1, (RHS, 128))
    be1 = jnp.broadcast_to(beta1, (RHS, 128))
    k0 = jnp.broadcast_to(alpha0 + alpha1 * beta1, (RHS, 128))

    def update1(e, carry):
        u = u1[e] - (al1 * m1[e] + ab1 * m0[e])
        w = w1[e] - (al1 * n1[e] + ab1 * n0[e])
        r = r0[e] - (k0 * w0[e] + al1 * w1[e])
        m1[e] = u
        n1[e] = w
        return carry[0] + r * u, carry[1] + w * u

    value = dot_pack(*lax.fori_loop(0, ROWS, update1, (zero, zero), unroll=16))
    dot_start(2, 0, value)

    def prepare(e):
        u, w = u0[e], w0[e]
        v, q = u1[e], w1[e]
        return k0 * u + al1 * v, m1[e], v + be1 * u, r0[e] - (k0 * w + al1 * q), n1[e], q + be1 * w

    def prepare_pair(j):
        for k, (a, b) in enumerate(zip(prepare(inverse[0, 2 * j]), prepare(inverse[0, 2 * j + 1]))):
            parts[k, j] = jnp.where(left, a, b)

    loop(0, ROWS // 2, prepare_pair, 8)
    parts_copy = pltpu.make_async_copy(parts, parts_hbm, out_sem.at[0])
    parts_copy.start()
    dot_start(2, 1, dot_finish(2, 0))
    gam2, del2 = dot_unpack(dot_finish(2, 1))
    beta2 = gam2 / gam1
    alpha2 = gam2 / (del2 - beta2 * gam2 / alpha1)
    coef[0] = jnp.broadcast_to(alpha2, (RHS, 128))
    coef[1] = jnp.broadcast_to(alpha2 * beta2, (RHS, 128))
    coef_copy = pltpu.make_async_copy(coef, coef_hbm, out_sem.at[1])
    coef_copy.start()
    parts_copy.wait()
    coef_copy.wait()

    g0_copy().wait_send()
    for slot in range(12):
        if slot != 1:
            halo_copy(slot).wait_send()
    for number in range(3):
        for stage in range(2):
            slots = dot_slots(number, stage)
            pltpu.make_async_copy(slots, slots, dot_ssem.at[number, stage]).wait()


def finish(parts_hbm, coef_hbm, x_hbm, r_hbm, parts, coef, x_out, r_out, in_sem, coef_sem, out_sem):
    size = ROWS // 2 // LAST_CHUNKS
    coef_copy = pltpu.make_async_copy(coef_hbm, coef, coef_sem)
    coef_copy.start()
    copies = []
    for c in range(LAST_CHUNKS):
        part = pl.ds(c * size, size)
        copies.append(pltpu.make_async_copy(parts_hbm.at[:, part], parts.at[:, part], in_sem.at[c]))
        copies[-1].start()
    coef_copy.wait()
    alpha, alpha_beta = coef[0], coef[1]
    ends = []
    for c in range(LAST_CHUNKS):
        copies[c].wait()

        def one(j):
            x = parts[0, j] + (alpha * parts[1, j] + alpha_beta * parts[2, j])
            r = parts[3, j] - (alpha * parts[4, j] + alpha_beta * parts[5, j])
            for ref, v in ((x_out, x), (r_out, r)):
                ref[2 * j] = v[:, :DOFS]
                ref[2 * j + 1] = v[:, DOFS:]

        loop(c * size, (c + 1) * size, one)
        rows = pl.ds(2 * c * size, 2 * size)
        for k, (ref, hbm) in enumerate(((x_out, x_hbm), (r_out, r_hbm))):
            ends.append(pltpu.make_async_copy(ref.at[rows], hbm.at[rows], out_sem.at[k, c]))
            ends[-1].start()
    for c in ends:
        c.wait()


def body(right_side, a_blocks, a_cols, g_blocks, g_cols, send_up, send_down):
    field = pltpu.VMEM((ROWS, RHS, 128), F32)
    packed = pltpu.VMEM((ROWS, 2 * RHS, 128), BF16)
    edge = pltpu.VMEM((FACE, RHS, 128), F32)
    face = pltpu.VMEM((FACE, 2 * RHS, 128), BF16)
    hbm = pl.BlockSpec(memory_space=pl.ANY)
    smem = pl.BlockSpec(memory_space=pltpu.SMEM)
    dma = pltpu.SemaphoreType.DMA
    pairs = FACE // 2
    parts, coef = pl.pallas_call(
        kernel,
        out_shape=(jax.ShapeDtypeStruct((6, ROWS // 2, RHS, 128), F32), jax.ShapeDtypeStruct((2, RHS, 128), F32)),
        in_specs=[hbm, hbm, hbm, smem, smem, smem],
        out_specs=(hbm, hbm),
        scratch_shapes=[
            pltpu.VMEM((ROWS, RHS, DOFS), F32),
            pltpu.VMEM((A_SLOTS, A_CHUNK, 7, DOFS, DOFS), F32),
            pltpu.VMEM((ROWS, 4, DOFS, DOFS), F32),
            pltpu.VMEM((ROWS * 7, DOFS, 128), BF16),
            pltpu.VMEM((ROWS * 4, DOFS, 128), BF16),
            pltpu.VMEM((FACE, DOFS, 128), BF16),
            pltpu.VMEM((FACE * 3, DOFS, 128), BF16),
            packed, packed, packed,
            face, face, face, face,
            edge, edge, edge, edge,
            field, field, field, field, field, field, field, field, field,
            pltpu.VMEM((6, ROWS // 2, RHS, 128), F32),
            pltpu.VMEM((2, RHS, 128), F32),
            pltpu.VMEM((pairs, DOFS, 128), F32),
            pltpu.VMEM((pairs, DOFS, 128), F32),
            pltpu.VMEM((pairs * 3, DOFS, 128), F32),
            pltpu.VMEM((pairs * 3, DOFS, 128), F32),
            pltpu.VMEM((12, FACE // 2, RHS, 128), F32),
            pltpu.VMEM((12, FACE // 2, RHS, 128), F32),
            pltpu.VMEM((3, 2, 1, 128), F32),
            pltpu.VMEM((3, FIRST_SLOT[2], 1, 128), F32),
            pltpu.SMEM((ROWS,), jnp.int32),
            pltpu.SMEM((8, 128), jnp.int32),
            pltpu.SMEM((ROWS * 4,), jnp.int32),
            pltpu.SMEM((FACE,), jnp.int32),
            pltpu.SMEM((FACE,), jnp.int32),
            pltpu.SMEM((2 * FACE,), jnp.int32),
            pltpu.VMEM((8, 128), jnp.int32),
            dma((5,)), dma((A_SLOTS,)), dma((2,)), dma, dma, dma, dma, dma,
            dma((12,)), dma((12,)), dma((3, 2)), dma((3, 2)),
        ],
        compiler_params=pltpu.CompilerParams(
            collective_id=0, has_side_effects=True, vmem_limit_bytes=60 * 2 ** 20),
    )(right_side, a_blocks, g_blocks, a_cols.T, send_up, send_down)
    out = jax.ShapeDtypeStruct((ROWS, RHS, DOFS), F32)
    return pl.pallas_call(
        finish,
        out_shape=(out, out),
        in_specs=[hbm, hbm],
        out_specs=(hbm, hbm),
        scratch_shapes=[
            pltpu.VMEM((6, ROWS // 2, RHS, 128), F32),
            pltpu.VMEM((2, RHS, 128), F32),
            pltpu.VMEM((ROWS, RHS, DOFS), F32),
            pltpu.VMEM((ROWS, RHS, DOFS), F32),
            dma((LAST_CHUNKS,)), dma, dma((2, LAST_CHUNKS)),
        ],
        compiler_params=pltpu.CompilerParams(vmem_limit_bytes=60 * 2 ** 20),
    )(parts, coef)


def solution(mesh):
    in_specs = (
        P("dom", None, None),
        P("dom", None, None, None),
        P("dom", None),
        P("dom", None, None, None),
        P("dom", None),
        P("dom", None),
        P("dom", None),
    )
    out_specs = (P("dom", None, None), P("dom", None, None))
    return jax.shard_map(body, mesh=mesh, in_specs=in_specs, out_specs=out_specs, check_vma=False)
```

```python
import itertools

import jax
import jax.numpy as jnp
from jax import lax
from jax.experimental import pallas as pl
from jax.experimental.pallas import tpu as pltpu
from jax.sharding import PartitionSpec as P

ROWS = 64
FACE = 16
LAYERS = 4
RHS = 32
DOFS = 64
MESH = pl.DeviceIdType.MESH
NT = (((1,), (1,)), ((), ()))
F32 = jnp.float32
BF16 = jnp.bfloat16
G_CHUNK = 16
A_CHUNK = 8
A_SLOTS = 4
GROUPS = (((1, 2), (8, 8)), ((2, 4), (64, 4)))
FIRST_SLOT = (0, 15, 30)
LAST_CHUNKS = 4


def loop(lo, hi, fn, unroll=None):
    def step(i, carry):
        fn(i)
        return carry

    lax.fori_loop(lo, hi, step, 0, unroll=(hi - lo) if unroll is None else unroll)


def kernel(rhs_hbm, a_hbm, g_hbm, cols, send_up, send_down, parts_hbm, coef_hbm,
           rhs_in, a_in, g_in, a_w, g_w, gz_w, g0_w, packed_w, packed_y, packed_m,
           low_w, high_y, low_m, high_m, y_loc, y_far, u_low, u_high,
           r0, u0, w0, m0, n0, u1, w1, m1, n1, parts, coef,
           gz_send, gz_recv, g0_send, g0_recv, halo_send, halo_recv, dot_send, dot_recv,
           place, inverse, near, low_at, high_at, high_side, inverse_vec,
           in_sem, a_sem, out_sem, tab_sem, gz_ssem, gz_rsem, g0_ssem, g0_rsem, halo_ssem, halo_rsem, dot_ssem, dot_rsem):
    count = lax.axis_size("dom")
    me = lax.axis_index("dom")
    above = lax.rem(me + 1, count)
    below = lax.rem(me + count - 1, count)

    def partners(stage):
        out = []
        for steps in itertools.product(*[range(size) for _, size in GROUPS[stage]]):
            device = me
            for (stride, size), step in zip(GROUPS[stage], steps):
                if step:
                    mine = lax.rem(me // stride, size)
                    device = device + (lax.rem(mine + step, size) - mine) * stride
            if any(steps):
                out.append(device)
        return out

    def rhs_copy():
        return pltpu.make_async_copy(rhs_hbm, rhs_in, in_sem.at[0])

    def g_copy(c):
        part = pl.ds(c * G_CHUNK, G_CHUNK)
        return pltpu.make_async_copy(g_hbm.at[part], g_in.at[part], in_sem.at[1 + c])

    def a_copy(c):
        return pltpu.make_async_copy(a_hbm.at[pl.ds(c * A_CHUNK, A_CHUNK)], a_in.at[c % A_SLOTS], a_sem.at[c % A_SLOTS])

    rhs_copy().start()
    for c in range(ROWS // G_CHUNK):
        g_copy(c).start()
    for c in range(A_SLOTS):
        a_copy(c).start()

    barrier = pltpu.get_barrier_semaphore()
    greeted = 2
    for device in (above, below):
        pl.semaphore_signal(barrier, inc=1, device_id=(device,), device_id_type=MESH)
    for stage in range(2):
        for device in partners(stage):
            pl.semaphore_signal(barrier, inc=1, device_id=(device,), device_id_type=MESH)
            greeted += 1

    def first_layer(h):
        place[h] = send_down[0, h]

    loop(0, FACE, first_layer)

    def next_layer(e):
        place[e + FACE] = cols[5, place[e]]

    loop(0, ROWS - FACE, next_layer, 1)
    tab_lane = lax.broadcasted_iota(jnp.int32, (8, 128), 1)
    vec = lax.fori_loop(0, ROWS, lambda e, v: jnp.where(tab_lane == place[e], e, v),
                        jnp.zeros((8, 128), jnp.int32), unroll=8)
    inverse_vec[...] = vec
    tab = pltpu.make_async_copy(inverse_vec, inverse, tab_sem)
    tab.start()
    tab.wait()

    def neighbours(e):
        row = place[e]
        for k in range(4):
            near[e * 4 + k] = inverse[0, cols[k, row]]

    loop(0, ROWS, neighbours, 4)

    def crossings(h):
        low_at[h] = jnp.clip(cols[4, place[h]] - ROWS, 0, FACE - 1)
        high_at[h] = jnp.clip(cols[5, place[3 * FACE + h]] - (ROWS + FACE), 0, FACE - 1)

        for s in range(2):
            high_side[h * 2 + s] = jnp.clip(near[(3 * FACE + h) * 4 + 1 + 2 * s] - 3 * FACE, 0, FACE - 1)

    loop(0, FACE, crossings, 4)

    left = lax.broadcasted_iota(jnp.int32, (RHS, 128), 1) < DOFS
    left2 = lax.broadcasted_iota(jnp.int32, (2 * RHS, 128), 1) < DOFS

    def twice(v):
        return jnp.concatenate([v, v], axis=1)

    def split(ref, e, v):
        hi = v.astype(BF16)
        ref[e, 0:RHS] = hi
        ref[e, RHS:2 * RHS] = (v - hi.astype(F32)).astype(BF16)

    def split_block(v):
        hi = v.astype(BF16)
        lo = (v - hi.astype(F32)).astype(BF16)
        return jnp.concatenate([hi, lo], axis=1)

    def times(fields, weights):
        out = lax.dot_general(jnp.concatenate(fields, axis=1), jnp.concatenate(weights, axis=1), NT,
                              preferred_element_type=F32)
        return out[:RHS] + out[RHS:]

    def times_transposed(fields, weights):
        pair = [jnp.where(left2, fields[i], fields[i + 1]) for i in range(0, len(fields) - 1, 2)]
        if len(fields) % 2:
            pair.append(fields[-1][:, :DOFS])
        out = jnp.dot(jnp.concatenate(pair, axis=1), jnp.concatenate(weights, axis=0), preferred_element_type=F32)
        out = out[:RHS] + out[RHS:]
        return out + pltpu.roll(out, DOFS, 1)

    def convert_g(c):
        def one(b):
            i = c * G_CHUNK + b // 4
            k = b % 4
            g_w[i * 4 + k] = split_block(g_in[i, k])

        loop(0, G_CHUNK * 4, one)

    def convert_a(c):
        a_copy(c).wait()
        slot = c % A_SLOTS

        def one(i):
            for k in range(7):
                a_w[(c * A_CHUNK + i) * 7 + k] = split_block(a_in[slot, i, k])

        loop(0, A_CHUNK, one)
        if c + A_SLOTS < ROWS // A_CHUNK:
            a_copy(c + A_SLOTS).start()

    def halo_copy(slot):
        return pltpu.make_async_remote_copy(
            src_ref=halo_send.at[slot], dst_ref=halo_recv.at[slot], send_sem=halo_ssem.at[slot],
            recv_sem=halo_rsem.at[slot], device_id=(above if slot % 2 == 0 else below,), device_id_type=MESH)

    def send_top(slot, field):
        def one(j):
            halo_send[slot, j] = jnp.where(left, field[inverse[0, send_up[0, 2 * j]]],
                                           field[inverse[0, send_up[0, 2 * j + 1]]])

        loop(0, FACE // 2, one)
        halo_copy(slot).start()

    def send_bottom(slot, field):
        def one(j):
            halo_send[slot, j] = jnp.where(left, field[2 * j], field[2 * j + 1])

        loop(0, FACE // 2, one)
        halo_copy(slot).start()

    def halves(v):
        turned = pltpu.roll(v, DOFS, 1)
        return jnp.where(left, v, turned), jnp.where(left, turned, v)

    def unpack(slot, ref):
        def one(j):
            ref[2 * j], ref[2 * j + 1] = halves(halo_recv[slot, j])

        loop(0, FACE // 2, one)

    def unpack_split(slot, ref):
        def one(j):
            first, second = halves(halo_recv[slot, j])
            split(ref, 2 * j, first)
            split(ref, 2 * j + 1, second)

        loop(0, FACE // 2, one)

    def row_y(e, below_block):
        row = place[e] * 4
        return times([packed_w[e], packed_w[near[e * 4]], packed_w[near[e * 4 + 2]], below_block],
                     [g_w[row], g_w[row + 1], g_w[row + 2], g_w[row + 3]])

    def row_u(e, above_block, above_weight):
        ex = near[e * 4 + 1]
        ey = near[e * 4 + 3]
        return times_transposed(
            [packed_y[e], packed_y[ex], packed_y[ey], above_block],
            [g_w[place[e] * 4], g_w[place[ex] * 4 + 1], g_w[place[ey] * 4 + 2], above_weight])

    def row_a(e, below_block, above_block):
        row = place[e] * 7
        return twice(times(
            [packed_m[e]] + [packed_m[near[e * 4 + k]] for k in range(4)] + [below_block, above_block],
            [a_w[row + k] for k in range(7)]))

    def bottom(h):
        row = place[h] * 4
        y_loc[h] = twice(times([packed_w[h], packed_w[near[h * 4]], packed_w[near[h * 4 + 2]]],
                               [g_w[row], g_w[row + 1], g_w[row + 2]]))

    def inner_y(e):
        split(packed_y, e, twice(row_y(e, packed_w[e - FACE])))

    def first_product(out_m, out_n, beside_first, beside_inner, beside_second):
        loop(0, FACE, bottom)
        send_bottom(1, y_loc)
        beside_first()
        loop(FACE, ROWS, inner_y)

        def put_u(e, v):
            out_m[e] = v
            split(packed_m, e, v)

        def inner_u(e):
            put_u(e, row_u(e, packed_y[e + FACE], g_w[place[e + FACE] * 4 + 3]))

        loop(FACE, 3 * FACE, inner_u)

        halo_copy(0).wait_recv()
        unpack_split(0, low_w)

        def close_y_low(h):
            extra = times([low_w[low_at[h]]], [g_w[place[h] * 4 + 3]])
            split(packed_y, h, y_loc[h] + twice(extra))

        def outer_u_low(h):
            put_u(h, row_u(h, packed_y[h + FACE], g_w[place[h + FACE] * 4 + 3]))

        loop(0, FACE, close_y_low)
        loop(0, FACE, outer_u_low)
        send_bottom(3, out_m)
        beside_inner()
        halo_copy(1).wait_recv()
        unpack(1, y_far)

        def close_y_high(h):
            t = high_at[h]
            more = times([packed_w[3 * FACE + h]], [gz_w[t]])
            split(high_y, h, y_far[t] + twice(more))

        def outer_u_high(h):
            e = 3 * FACE + h
            put_u(e, row_u(e, high_y[h], gz_w[high_at[h]]))

        loop(0, FACE, close_y_high)
        loop(0, FACE, outer_u_high)
        send_top(2, out_m)
        beside_second()

        def inner_a(e):
            out_n[e] = row_a(e, packed_m[e - FACE], packed_m[e + FACE])

        def outer_a_high(h):
            e = 3 * FACE + h
            out_n[e] = row_a(e, packed_m[e - FACE], high_m[high_at[h]])

        def outer_a_low(h):
            out_n[h] = row_a(h, low_m[low_at[h]], packed_m[h + FACE])

        loop(FACE, 3 * FACE, inner_a)
        halo_copy(3).wait_recv()
        unpack_split(3, high_m)
        loop(0, FACE, outer_a_high)
        send_top(4, out_n)
        halo_copy(2).wait_recv()
        unpack_split(2, low_m)
        loop(0, FACE, outer_a_low)

    def later_product(number, out_m, out_n, start_sum, beside, before_high):
        base = number * 4

        def part_high(h):
            e = 3 * FACE + h
            ex = near[e * 4 + 1]
            ey = near[e * 4 + 3]
            out_m[e] = times_transposed([packed_y[e], packed_y[ex], packed_y[ey]],
                                        [g_w[place[e] * 4], g_w[place[ex] * 4 + 1], g_w[place[ey] * 4 + 2]])

        def part_low(h):
            out_m[h] = times_transposed([packed_y[h + FACE]], [g_w[place[h + FACE] * 4 + 3]])

        start_sum()
        loop(3 * FACE, ROWS, inner_y)
        loop(0, FACE, part_high)
        send_top(base + 2, out_m)
        loop(0, FACE, bottom)
        send_bottom(base + 1, y_loc)
        loop(FACE, 2 * FACE, inner_y)
        loop(0, FACE, part_low)
        send_bottom(base + 3, out_m)
        loop(2 * FACE, 3 * FACE, inner_y)

        def put_u(e, v):
            out_m[e] = v
            split(packed_m, e, v)

        def inner_u(e):
            put_u(e, row_u(e, packed_y[e + FACE], g_w[place[e + FACE] * 4 + 3]))

        loop(FACE, 3 * FACE, inner_u)

        def part_a(h):
            for layer, k, other in ((1, 6, 2), (2, 5, 1)):
                e = layer * FACE + h
                row = place[e] * 7
                out_n[e] = twice(times(
                    [packed_m[e]] + [packed_m[near[e * 4 + i]] for i in range(4)] + [packed_m[other * FACE + h]],
                    [a_w[row + i] for i in range(5)] + [a_w[row + k]]))

        loop(0, FACE, part_a)
        beside()

        halo_copy(base).wait_recv()
        unpack_split(base, low_w)
        halo_copy(base + 2).wait_recv()
        unpack(base + 2, u_low)

        def close_y_low(h):
            extra = twice(times([low_w[low_at[h]]], [g_w[place[h] * 4 + 3]]))
            split(packed_y, h, y_loc[h] + extra)

        def close_u_low(h):
            ex, ey = near[h * 4 + 1], near[h * 4 + 3]
            put_u(h, out_m[h] + times_transposed(
                [packed_y[h], packed_y[ex], packed_y[ey]],
                [g_w[place[h] * 4], g_w[place[ex] * 4 + 1], g_w[place[ey] * 4 + 2]]))
            split(low_m, h, u_low[low_at[h]] + times_transposed([packed_y[h]], [g_w[place[h] * 4 + 3]]))

        def close_a_low(h):
            out_n[h] = row_a(h, low_m[h], packed_m[h + FACE])
            e = FACE + h
            out_n[e] = out_n[e] + twice(times([packed_m[h]], [a_w[place[e] * 7 + 5]]))

        loop(0, FACE, close_y_low)
        loop(0, FACE, close_u_low)
        loop(0, FACE, close_a_low)

        before_high()

        halo_copy(base + 1).wait_recv()
        halo_copy(base + 3).wait_recv()
        unpack(base + 1, y_far)
        unpack(base + 3, u_high)

        def close_y_high(h):
            more = twice(times([packed_w[3 * FACE + h]], [gz_w[high_at[h]]]))
            split(high_y, h, y_far[high_at[h]] + more)

        def close_u_high(h):
            e = 3 * FACE + h
            put_u(e, out_m[e] + times_transposed([high_y[h]], [gz_w[high_at[h]]]))
            hx, hy = high_side[2 * h], high_side[2 * h + 1]
            split(high_m, h, u_high[high_at[h]] + times_transposed(
                [high_y[h], high_y[hx], high_y[hy]],
                [g0_w[high_at[h] * 3], g0_w[high_at[hx] * 3 + 1], g0_w[high_at[hy] * 3 + 2]]))

        def close_a_high(h):
            e = 3 * FACE + h
            out_n[e] = row_a(e, packed_m[e - FACE], high_m[h])
            e = 2 * FACE + h
            out_n[e] = out_n[e] + twice(times([packed_m[e + FACE]], [a_w[place[e] * 7 + 6]]))

        loop(0, FACE, close_y_high)
        loop(0, FACE, close_u_high)
        loop(0, FACE, close_a_high)

    dot_lane = lax.broadcasted_iota(jnp.int32, (RHS, 128), 1)
    dot_row = lax.broadcasted_iota(jnp.int32, (RHS, 128), 0)

    def dot_slots(number, stage):
        return dot_recv.at[number, pl.ds(FIRST_SLOT[stage], FIRST_SLOT[stage + 1] - FIRST_SLOT[stage])]

    def dot_start(number, stage, value):
        dot_send[number, stage] = value
        for i, device in enumerate(partners(stage)):
            pltpu.make_async_remote_copy(
                src_ref=dot_send.at[number, stage], dst_ref=dot_recv.at[number, FIRST_SLOT[stage] + i],
                send_sem=dot_ssem.at[number, stage], recv_sem=dot_rsem.at[number, stage],
                device_id=(device,), device_id_type=MESH).start()

    def dot_finish(number, stage):
        slots = dot_slots(number, stage)
        pltpu.make_async_copy(slots, slots, dot_rsem.at[number, stage]).wait()
        got = dot_recv[number, FIRST_SLOT[stage]:FIRST_SLOT[stage + 1]]
        return dot_send[number, stage] + jnp.sum(got, axis=0)

    def dot_pack(first, second):
        first = jnp.sum(first, axis=1, keepdims=True)
        second = jnp.sum(second, axis=1, keepdims=True)
        spread = jnp.where(dot_lane == dot_row, first, jnp.where(dot_lane == dot_row + RHS, second, 0.0))
        return jnp.sum(spread, axis=0, keepdims=True)

    def dot_unpack(v):
        first = jnp.sum(jnp.where(dot_lane == dot_row, v, 0.0), axis=1, keepdims=True)
        second = jnp.sum(jnp.where(dot_lane == dot_row + RHS, v, 0.0), axis=1, keepdims=True)
        return first, second

    zero = jnp.zeros((RHS, 128), F32)

    rhs_copy().wait()

    def load_rhs(e):
        v = twice(rhs_in[place[e]])
        r0[e] = v
        split(packed_w, e, v)

    loop(0, ROWS, load_rhs, 16)
    pl.semaphore_wait(barrier, greeted)
    send_top(0, r0)

    def gz_copy():
        return pltpu.make_async_remote_copy(src_ref=gz_send, dst_ref=gz_recv, send_sem=gz_ssem, recv_sem=gz_rsem,
                                            device_id=(below,), device_id_type=MESH)

    def g0_copy():
        return pltpu.make_async_remote_copy(src_ref=g0_send, dst_ref=g0_recv, send_sem=g0_ssem, recv_sem=g0_rsem,
                                            device_id=(below,), device_id_type=MESH)

    def fill_gz(j):
        gz_send[j] = jnp.concatenate([g_in[place[2 * j], 3], g_in[place[2 * j + 1], 3]], axis=1)

    def fill_g0(j):
        pair = [g_in[place[(2 * j + s) // 3], (2 * j + s) % 3] for s in range(2)]
        g0_send[j] = jnp.concatenate(pair, axis=1)

    def split_pairs(received, ref, pairs):
        def one(j):
            v = received[j]
            ref[2 * j] = split_block(v[:, :DOFS])
            ref[2 * j + 1] = split_block(v[:, DOFS:])

        loop(0, pairs, one)

    chunks = ROWS // G_CHUNK
    for c in range(chunks):
        g_copy(c).wait()
        if c == chunks - 1:
            loop(0, FACE // 2, fill_gz)
            gz_copy().start()
        convert_g(c)

    def first_side():
        loop(0, FACE * 3 // 2, fill_g0)
        for c in range(4):
            convert_a(c)

    def inner_side():
        halo_copy(1).wait_send()
        gz_copy().wait_send()
        g0_copy().start()
        for c in range(4, 6):
            convert_a(c)
        gz_copy().wait_recv()
        split_pairs(gz_recv, gz_w, FACE // 2)

    def second_side():
        for c in range(6, ROWS // A_CHUNK):
            convert_a(c)

    first_product(u0, w0, first_side, inner_side, second_side)

    def dots0(e, carry):
        split(packed_w, e, w0[e])
        return carry[0] + r0[e] * u0[e], carry[1] + w0[e] * u0[e]

    sums0 = lax.fori_loop(0, ROWS, dots0, (zero, zero), unroll=16)

    def beside1():
        dot_start(0, 1, dot_finish(0, 0))

    def background():
        g0_copy().wait_recv()
        split_pairs(g0_recv, g0_w, FACE * 3 // 2)

    def nothing():
        pass

    def beside2():
        dot_start(1, 1, dot_finish(1, 0))

    later_product(1, m0, n0, lambda: dot_start(0, 0, dot_pack(*sums0)), beside1, background)
    gam0, del0 = dot_unpack(dot_finish(0, 1))
    alpha0 = gam0 / del0
    al0 = jnp.broadcast_to(alpha0, (RHS, 128))

    def update0(e, carry):
        u = u0[e] - al0 * m0[e]
        w = w0[e] - al0 * n0[e]
        r = r0[e] - al0 * w0[e]
        u1[e] = u
        w1[e] = w
        split(packed_w, e, w)
        return carry[0] + r * u, carry[1] + w * u

    sums = lax.fori_loop(3 * FACE, ROWS, update0, (zero, zero), unroll=16)
    send_top(8, w1)
    sums1 = lax.fori_loop(0, 3 * FACE, update0, sums, unroll=16)

    later_product(2, m1, n1, lambda: dot_start(1, 0, dot_pack(*sums1)), beside2, nothing)
    gam1, del1 = dot_unpack(dot_finish(1, 1))
    beta1 = gam1 / gam0
    alpha1 = gam1 / (del1 - beta1 * gam1 / alpha0)
    al1 = jnp.broadcast_to(alpha1, (RHS, 128))
    ab1 = jnp.broadcast_to(alpha1 * beta1, (RHS, 128))
    be1 = jnp.broadcast_to(beta1, (RHS, 128))
    k0 = jnp.broadcast_to(alpha0 + alpha1 * beta1, (RHS, 128))

    def update1(e, carry):
        u = u1[e] - (al1 * m1[e] + ab1 * m0[e])
        w = w1[e] - (al1 * n1[e] + ab1 * n0[e])
        r = r0[e] - (k0 * w0[e] + al1 * w1[e])
        m1[e] = u
        n1[e] = w
        return carry[0] + r * u, carry[1] + w * u

    value = dot_pack(*lax.fori_loop(0, ROWS, update1, (zero, zero), unroll=16))
    dot_start(2, 0, value)

    def prepare(e):
        u, w = u0[e], w0[e]
        v, q = u1[e], w1[e]
        return k0 * u + al1 * v, m1[e], v + be1 * u, r0[e] - (k0 * w + al1 * q), n1[e], q + be1 * w

    def prepare_pair(j):
        for k, (a, b) in enumerate(zip(prepare(inverse[0, 2 * j]), prepare(inverse[0, 2 * j + 1]))):
            parts[k, j] = jnp.where(left, a, b)

    loop(0, ROWS // 2, prepare_pair, 8)
    parts_copy = pltpu.make_async_copy(parts, parts_hbm, out_sem.at[0])
    parts_copy.start()
    dot_start(2, 1, dot_finish(2, 0))
    gam2, del2 = dot_unpack(dot_finish(2, 1))
    beta2 = gam2 / gam1
    alpha2 = gam2 / (del2 - beta2 * gam2 / alpha1)
    coef[0] = jnp.broadcast_to(alpha2, (RHS, 128))
    coef[1] = jnp.broadcast_to(alpha2 * beta2, (RHS, 128))
    coef_copy = pltpu.make_async_copy(coef, coef_hbm, out_sem.at[1])
    coef_copy.start()
    parts_copy.wait()
    coef_copy.wait()

    g0_copy().wait_send()
    for slot in range(12):
        if slot != 1:
            halo_copy(slot).wait_send()
    for number in range(3):
        for stage in range(2):
            slots = dot_slots(number, stage)
            pltpu.make_async_copy(slots, slots, dot_ssem.at[number, stage]).wait()


def finish(parts_hbm, coef_hbm, x_hbm, r_hbm, parts, coef, x_out, r_out, in_sem, coef_sem, out_sem):
    size = ROWS // 2 // LAST_CHUNKS
    coef_copy = pltpu.make_async_copy(coef_hbm, coef, coef_sem)
    coef_copy.start()
    copies = []
    for c in range(LAST_CHUNKS):
        part = pl.ds(c * size, size)
        copies.append(pltpu.make_async_copy(parts_hbm.at[:, part], parts.at[:, part], in_sem.at[c]))
        copies[-1].start()
    coef_copy.wait()
    alpha, alpha_beta = coef[0], coef[1]
    ends = []
    for c in range(LAST_CHUNKS):
        copies[c].wait()

        def one(j):
            x = parts[0, j] + (alpha * parts[1, j] + alpha_beta * parts[2, j])
            r = parts[3, j] - (alpha * parts[4, j] + alpha_beta * parts[5, j])
            for ref, v in ((x_out, x), (r_out, r)):
                ref[2 * j] = v[:, :DOFS]
                ref[2 * j + 1] = v[:, DOFS:]

        loop(c * size, (c + 1) * size, one)
        rows = pl.ds(2 * c * size, 2 * size)
        for k, (ref, hbm) in enumerate(((x_out, x_hbm), (r_out, r_hbm))):
            ends.append(pltpu.make_async_copy(ref.at[rows], hbm.at[rows], out_sem.at[k, c]))
            ends[-1].start()
    for c in ends:
        c.wait()


def body(right_side, a_blocks, a_cols, g_blocks, g_cols, send_up, send_down):
    field = pltpu.VMEM((ROWS, RHS, 128), F32)
    packed = pltpu.VMEM((ROWS, 2 * RHS, 128), BF16)
    edge = pltpu.VMEM((FACE, RHS, 128), F32)
    face = pltpu.VMEM((FACE, 2 * RHS, 128), BF16)
    hbm = pl.BlockSpec(memory_space=pl.ANY)
    smem = pl.BlockSpec(memory_space=pltpu.SMEM)
    dma = pltpu.SemaphoreType.DMA
    pairs = FACE // 2
    parts, coef = pl.pallas_call(
        kernel,
        out_shape=(jax.ShapeDtypeStruct((6, ROWS // 2, RHS, 128), F32), jax.ShapeDtypeStruct((2, RHS, 128), F32)),
        in_specs=[hbm, hbm, hbm, smem, smem, smem],
        out_specs=(hbm, hbm),
        scratch_shapes=[
            pltpu.VMEM((ROWS, RHS, DOFS), F32),
            pltpu.VMEM((A_SLOTS, A_CHUNK, 7, DOFS, DOFS), F32),
            pltpu.VMEM((ROWS, 4, DOFS, DOFS), F32),
            pltpu.VMEM((ROWS * 7, DOFS, 128), BF16),
            pltpu.VMEM((ROWS * 4, DOFS, 128), BF16),
            pltpu.VMEM((FACE, DOFS, 128), BF16),
            pltpu.VMEM((FACE * 3, DOFS, 128), BF16),
            packed, packed, packed,
            face, face, face, face,
            edge, edge, edge, edge,
            field, field, field, field, field, field, field, field, field,
            pltpu.VMEM((6, ROWS // 2, RHS, 128), F32),
            pltpu.VMEM((2, RHS, 128), F32),
            pltpu.VMEM((pairs, DOFS, 128), F32),
            pltpu.VMEM((pairs, DOFS, 128), F32),
            pltpu.VMEM((pairs * 3, DOFS, 128), F32),
            pltpu.VMEM((pairs * 3, DOFS, 128), F32),
            pltpu.VMEM((12, FACE // 2, RHS, 128), F32),
            pltpu.VMEM((12, FACE // 2, RHS, 128), F32),
            pltpu.VMEM((3, 2, 1, 128), F32),
            pltpu.VMEM((3, FIRST_SLOT[2], 1, 128), F32),
            pltpu.SMEM((ROWS,), jnp.int32),
            pltpu.SMEM((8, 128), jnp.int32),
            pltpu.SMEM((ROWS * 4,), jnp.int32),
            pltpu.SMEM((FACE,), jnp.int32),
            pltpu.SMEM((FACE,), jnp.int32),
            pltpu.SMEM((2 * FACE,), jnp.int32),
            pltpu.VMEM((8, 128), jnp.int32),
            dma((5,)), dma((A_SLOTS,)), dma((2,)), dma, dma, dma, dma, dma,
            dma((12,)), dma((12,)), dma((3, 2)), dma((3, 2)),
        ],
        compiler_params=pltpu.CompilerParams(
            collective_id=0, has_side_effects=True, vmem_limit_bytes=60 * 2 ** 20),
    )(right_side, a_blocks, g_blocks, a_cols.T, send_up, send_down)
    out = jax.ShapeDtypeStruct((ROWS, RHS, DOFS), F32)
    return pl.pallas_call(
        finish,
        out_shape=(out, out),
        in_specs=[hbm, hbm],
        out_specs=(hbm, hbm),
        scratch_shapes=[
            pltpu.VMEM((6, ROWS // 2, RHS, 128), F32),
            pltpu.VMEM((2, RHS, 128), F32),
            pltpu.VMEM((ROWS, RHS, DOFS), F32),
            pltpu.VMEM((ROWS, RHS, DOFS), F32),
            dma((LAST_CHUNKS,)), dma, dma((2, LAST_CHUNKS)),
        ],
        compiler_params=pltpu.CompilerParams(vmem_limit_bytes=60 * 2 ** 20),
    )(parts, coef)


def solution(mesh):
    in_specs = (
        P("dom", None, None),
        P("dom", None, None, None),
        P("dom", None),
        P("dom", None, None, None),
        P("dom", None),
        P("dom", None),
        P("dom", None),
    )
    out_specs = (P("dom", None, None), P("dom", None, None))
    return jax.shard_map(body, mesh=mesh, in_specs=in_specs, out_specs=out_specs, check_vma=False)
```
